128 devices in a mesh: region: 16 (over y, z), loop: 8 (over x, core).
Axes of the slice: x: 4, y: 4, z: 4, core: 2. Of those that a mesh axis runs over, the one named last changes fastest.
Arguments:
- tokens: bfloat16 [65536, 256], P(('region', 'loop')), may hold values from -6 to 6
- dest: int32 [65536, 1], P(('region', 'loop')), may hold values from 0 to 127; in each aligned block of 512 rows (0 to 511, 512 to 1023, ...) at most 8 rows name the same one
- norm1_gain: float32 [256], replicated, may hold values from 0.1 to 1.9
- w_qkv: bfloat16 [256, 768], replicated, may hold values from -0.8125 to 0.8125
- w_out: bfloat16 [256, 256], replicated, may hold values from -0.375 to 0.375
- norm2_gain: float32 [256], replicated, may hold values from 0.1 to 1.9
- w_hidden: bfloat16 [256, 1024], replicated, may hold values from -0.375 to 0.375
- w_back: bfloat16 [1024, 256], replicated, may hold values from -0.1875 to 0.1875
Outputs:
- updated: bfloat16 [65536, 256], P(('region', 'loop'))
The draws below stay inside these ranges and needn't reach their ends.
Inputs may be any that keep to these rules, and one draw needn't show every extreme that they name: `dest`: among the grains of one device, at most 8 have the same owner; in every draw some device sends exactly 8 grains to one owner. Every device is the owner of some grain.
All inputs are finite; a program needn't handle non-finite values.
Results may differ from the reference program's by a relative error of at most 0.011.
Values may be sent and summed in bfloat16 or wider, within the bound.
A program may use at most 128 MiB of HBM per device.

```python
import math
import jax
import jax.numpy as jnp
import numpy as np
from jax import lax

D = 256
HEADS = 8
FFN = 1024
ROWS = 512
HEAD_DIM = 32
CAP = 8
SLOTS = 1024
TOKENS = 65536
N_REGION = 16
N_LOOP = 8
DEVICES = 128


def draw_w_qkv(key, part):
    key = jax.random.fold_in(key, 7)
    first = jax.random.fold_in(key, 1)
    base = jax.random.truncated_normal(first, -4.0, 4.0, (D, 3 * D), jnp.float32) * D ** (-0.5)
    return base.astype(jnp.bfloat16)


def block_levels(own_key, extent, shards, smallest, largest):
    level = 1.0
    for position, parts in shards:
        draws = jax.random.uniform(jax.random.fold_in(jax.random.fold_in(own_key, 6), position), (parts,), jnp.float32, smallest / len(shards), largest / len(shards))
        level = level * jnp.repeat(jnp.exp(draws), extent[position] // parts).reshape((-1,) + (1,) * (len(extent) - 1 - position))
    return level


def assign_block(stream_key, own, number, rows, count, top, reach, lean):
    sequence = jax.random.permutation(stream_key, count)
    crowded, ordinary = shares(count, rows * top, reach, lean, True), shares(count, rows * top, reach, lean, False)
    places = jnp.arange(count)

    def named(tallies, offset_by):
        used = int((tallies > 0).sum())
        fixed = max(1, used // 4)
        passed = fixed + (places - fixed + offset_by * (used - fixed)) % max(1, count - fixed)
        return jnp.zeros((count,), jnp.int32).at[sequence[jnp.where(places < fixed, places, passed)]].set(jnp.asarray(tallies, jnp.int32))

    tallies = jnp.where(number % 4 == 0, named(crowded, number // 4), named(ordinary, number - number // 4 - 1))
    mixed = jax.random.permutation(jax.random.fold_in(own, 3), count)
    source_of, receiver = mixed[0:count // 2 * 2:2], mixed[1:count // 2 * 2:2]
    margin = jnp.minimum(tallies[source_of] - 1, reach - tallies[receiver]) // 2
    margin = jnp.where((source_of == sequence[0]) | (receiver == sequence[0]) | (tallies[receiver] == 0), 0, jnp.maximum(margin, 0))
    passed = jax.random.randint(jax.random.fold_in(own, 4), (count // 2,), 0, 1 << 20) % (margin + 1)
    tallies = tallies.at[source_of].add(-passed).at[receiver].add(passed)
    items = jnp.searchsorted(jnp.cumsum(tallies), jnp.arange(rows * top), side="right").astype(jnp.int32)
    grid = items.reshape(top, rows).T
    grid = grid[jax.random.permutation(jax.random.fold_in(own, 1), rows)]
    offset_by = jax.random.randint(jax.random.fold_in(own, 2), (rows, 1), 0, top)
    return jnp.take_along_axis(grid, (jnp.arange(top)[None, :] + offset_by) % top, axis=1)


def shares(count, total, bound, slope, full):
    weights = [(1 << 20) // math.isqrt(grade ** slope) + 1 for grade in range(1, count + 1)]
    largest = bound if full else min(bound, max(-(-total // count), total * weights[0] // sum(weights)))
    least = 1 if total - largest >= count - 1 else 0
    given, rest = [largest] + [least] * (count - 1), total - largest - least * (count - 1)
    while rest > 0:
        movable = [i for i in range(1, count) if given[i] < largest] or [i for i in range(1, count) if given[i] < bound]
        whole, remaining = sum([weights[i] for i in movable]), rest
        for i in movable:
            more = min(bound - given[i], max(1, remaining * weights[i] // whole), rest)
            given[i] = given[i] + more
            rest = rest - more
    return np.array(given)


def noise(own_key, shape, deviation, most, split=(), held_as=jnp.bfloat16):
    level = block_levels(own_key, shape, split, -0.22, 0.18) if split else 1.0
    values = jax.random.normal(own_key, shape, jnp.float32) * deviation * level
    return jnp.minimum(jnp.maximum(values, -most), most).astype(held_as)


def setup_inputs(seed: int = 0) -> dict:
    key_list = jax.random.split(jax.random.key(seed), 9)
    tokens = noise(key_list[0], (TOKENS, D), 1.0, 6.0, ((0, 128),))
    dest_keys = jax.random.split(jax.random.fold_in(key_list[1], 1), TOKENS // ROWS)
    dest_turns = jax.random.permutation(jax.random.fold_in(key_list[1], 3), TOKENS // ROWS)
    dest = jax.vmap(lambda own, number: assign_block(jax.random.fold_in(key_list[1], 2), own, number, ROWS, DEVICES, 1, CAP, 2))(dest_keys, dest_turns).reshape((TOKENS, 1))
    norm1_gain = jnp.clip(1.0 + 0.18 * jax.random.normal(key_list[2], (D,), jnp.float32), 0.1, 1.9)
    w_qkv = draw_w_qkv(jax.random.fold_in(key_list[8], 71), 0)
    w_out = noise(key_list[4], (D, D), D ** -0.5, 0.375)
    norm2_gain = jnp.clip(1.0 + 0.18 * jax.random.normal(key_list[5], (D,), jnp.float32), 0.1, 1.9)
    w_hidden = noise(key_list[6], (D, FFN), D ** -0.5, 0.375)
    w_back = noise(key_list[7], (FFN, D), FFN ** -0.5, 0.1875)
    return {"tokens": tokens, "dest": dest, "norm1_gain": norm1_gain, "w_qkv": w_qkv, "w_out": w_out, "norm2_gain": norm2_gain, "w_hidden": w_hidden, "w_back": w_back}


def layer_norm(values, gain):
    mean = lax.optimization_barrier(jnp.mean(values, axis=-1, keepdims=True))
    centered = values - mean
    variance = lax.optimization_barrier(jnp.mean(centered * centered, axis=-1, keepdims=True))
    return centered * lax.rsqrt(variance + 1e-05) * gain.astype(jnp.float32)

def reference(tokens, dest, norm1_gain, w_qkv, w_out, norm2_gain, w_hidden, w_back):
    target = dest[:, 0].reshape(DEVICES, ROWS)
    onehot = (target[:, :, None] == jnp.arange(DEVICES, dtype=jnp.int32)[None, None, :]).astype(jnp.int32)
    rank = lax.optimization_barrier(jnp.sum(jnp.cumsum(onehot, axis=1) * onehot, axis=2)) - 1
    source = jnp.arange(DEVICES, dtype=jnp.int32)[:, None]
    slot = (source * CAP + rank).reshape(-1).astype(jnp.int32)
    owner = target.reshape(-1).astype(jnp.int32)
    received = jnp.zeros((DEVICES, SLOTS, D), jnp.bfloat16).at[owner, slot].set(tokens)
    live = jnp.zeros((DEVICES, SLOTS), jnp.bool_).at[owner, slot].set(True)
    flat = received.reshape(DEVICES * SLOTS, D).astype(jnp.float32)
    normed = layer_norm(flat, norm1_gain).astype(jnp.bfloat16)
    projected = lax.optimization_barrier(jnp.dot(normed, w_qkv, preferred_element_type=jnp.float32).astype(jnp.bfloat16))
    queries = projected[:, :D].reshape(DEVICES, SLOTS, HEADS, HEAD_DIM)
    keys = projected[:, D:2 * D].reshape(N_REGION, N_LOOP * SLOTS, HEADS, HEAD_DIM)
    values = projected[:, 2 * D:].reshape(N_REGION, N_LOOP * SLOTS, HEADS, HEAD_DIM)
    key_live = live.reshape(N_REGION, N_LOOP * SLOTS)
    scale = 1.0 / HEAD_DIM ** 0.5

    def one_device(device):
        region = device // N_LOOP
        query_block = queries[device].astype(jnp.float32)
        key_block = keys[region].astype(jnp.float32)
        value_block = values[region].astype(jnp.float32)
        flags = key_live[region][None, None, :]
        scores = jnp.einsum('qhe,khe->qhk', query_block, key_block) * scale
        masked = jnp.where(flags, scores, -1e+30)
        top = lax.optimization_barrier(jnp.max(masked, axis=2, keepdims=True))
        weights = jnp.where(flags, jnp.exp(masked - top), 0.0)
        total = lax.optimization_barrier(jnp.sum(weights, axis=2))
        rounded = lax.optimization_barrier(weights.astype(jnp.bfloat16)).astype(jnp.float32)
        summed = jnp.einsum('qhk,khe->qhe', rounded, value_block) / total[:, :, None]
        return summed.reshape(SLOTS, D).astype(jnp.bfloat16)
    attended = lax.map(one_device, jnp.arange(DEVICES, dtype=jnp.int32)).reshape(DEVICES * SLOTS, D)
    mixed = flat + jnp.dot(attended, w_out, preferred_element_type=jnp.float32)
    normed2 = layer_norm(mixed, norm2_gain).astype(jnp.bfloat16)
    hidden = jax.nn.gelu(jnp.dot(normed2, w_hidden, preferred_element_type=jnp.float32), approximate=False).astype(jnp.bfloat16)
    result = (mixed + jnp.dot(hidden, w_back, preferred_element_type=jnp.float32)).astype(jnp.bfloat16)
    result = result.reshape(DEVICES, SLOTS, D)
    return result[owner, slot]
```

```python
import functools
import math

import jax
import jax.numpy as jnp
from jax import lax
from jax.experimental import pallas as pl
from jax.experimental.pallas import tpu as pltpu
from jax.sharding import PartitionSpec as P

HEADS = 8
CAP = 8
MARK = 16.0
MESH = pl.DeviceIdType.MESH
EXTRA = 16
F32 = jnp.float32
BF16 = jnp.bfloat16


def iota(shape, dim):
    return lax.broadcasted_iota(jnp.int32, shape, dim)


def one_hot(condition):
    return jnp.where(condition, 1.0, 0.0).astype(BF16)


def route_kernel(
    regions, loops, tokens_ref, dest_ref, pool_ref, place_ref, rank_ref,
    outbox, inbox, packed, send_a, recv_a, send_g, recv_g, local_sem,
):
    rows, width = tokens_ref.shape
    chunk = CAP * loops
    slots = regions * chunk
    chips = loops // 2
    region, loop = lax.axis_index("region"), lax.axis_index("loop")
    chip, core = loop // 2, lax.rem(loop, 2)
    sibling = chip * 2 + (1 - core)
    right = lax.rem(chip + 1, chips) * 2 + core
    left = lax.rem(chip + chips - 1, chips) * 2 + core
    far = lax.rem(chip + 2, chips) * 2 + core

    barrier = pltpu.get_barrier_semaphore()
    for k in range(1, regions):
        pl.semaphore_signal(
            barrier, inc=1, device_id=(lax.rem(region + k, regions), loop), device_id_type=MESH
        )
    for peer in (sibling, left, right):
        pl.semaphore_signal(barrier, inc=1, device_id=(region, peer), device_id_type=MESH)

    owner_region = dest_ref[...] // loops
    hot = one_hot(owner_region == iota((regions, rows), 0))
    upper = one_hot(iota((rows, rows), 0) <= iota((rows, rows), 1))
    before = jnp.dot(hot, upper, preferred_element_type=F32)
    rank = jnp.sum(before * hot.astype(F32), axis=0, keepdims=True).astype(jnp.int32) - 1
    place = owner_region * chunk + rank
    place_ref[...] = jnp.broadcast_to(place, place_ref.shape)
    spread = one_hot(iota((slots, rows), 0) == place)
    sorted_rows = jnp.dot(spread, tokens_ref[...], preferred_element_type=F32)
    held = jnp.dot(spread, jnp.ones((rows, width), BF16), preferred_element_type=F32)
    outbox[...] = (sorted_rows + (1.0 - held) * MARK).astype(BF16)

    pl.semaphore_wait(barrier, regions - 1 + 3)

    def exchange(k):
        peer = lax.rem(region + k, regions)
        return pltpu.make_async_remote_copy(
            src_ref=outbox.at[pl.ds(pl.multiple_of(peer * chunk, chunk), chunk)],
            dst_ref=inbox.at[pl.ds(pl.multiple_of(region * chunk, chunk), chunk)],
            send_sem=send_a.at[k],
            recv_sem=recv_a.at[k],
            device_id=(peer, loop),
            device_id_type=MESH,
        )

    exchanges = [exchange(k) for k in range(1, regions)]
    for copy in exchanges:
        copy.start()
    own = pl.ds(pl.multiple_of(region * chunk, chunk), chunk)
    inbox[own, :] = outbox[own, :]
    earlier = one_hot(iota((slots, slots), 0) < iota((slots, slots), 1))
    for copy in exchanges:
        copy.wait_recv()

    alive = jnp.where(inbox[:, :128].astype(F32) < 8.0, 1.0, 0.0)
    alive_row = alive.T[:16, :]
    ahead = jnp.dot(alive_row.astype(BF16), earlier, preferred_element_type=F32)
    slot = jnp.where(alive_row > 0.0, ahead, -1.0).astype(jnp.int32)
    rank_ref[...] = slot[:8, :]
    squeeze = one_hot(iota((slots, slots), 0) == slot[0:1, :])
    packed[pl.ds(0, slots), :] = jnp.dot(
        squeeze, inbox[...], preferred_element_type=F32
    ).astype(BF16)
    count = jnp.sum(alive_row, axis=1, keepdims=True)
    high = jnp.floor(count * (1.0 / 128.0))
    packed[pl.ds(slots, EXTRA), :] = jnp.where(
        iota((EXTRA, width), 1) < 128, high, count - 128.0 * high
    ).astype(BF16)

    half0, half1 = pl.ds(0, slots // 2), pl.ds(slots // 2, slots // 2 + EXTRA)
    whole = pl.ds(0, slots + EXTRA)

    def move(n, src, slot_index, part, peer):
        copy = pltpu.make_async_remote_copy(
            src_ref=src.at[part],
            dst_ref=pool_ref.at[slot_index, part],
            send_sem=send_g.at[n],
            recv_sem=recv_g.at[n],
            device_id=(region, peer),
            device_id_type=MESH,
        )
        copy.start()
        return copy

    started = [
        move(0, packed, loop, half0, right),
        move(1, packed, loop, half1, left),
        move(2, packed, loop, half1, right),
        move(3, packed, loop, half0, left),
        move(4, packed, loop, whole, sibling),
    ]
    keep = pltpu.make_async_copy(packed, pool_ref.at[loop], local_sem)
    keep.start()
    started[0].wait_recv()
    started.append(move(5, pool_ref.at[left], left, half0, right))
    started.append(move(6, pool_ref.at[left], left, half0, sibling))
    started[1].wait_recv()
    started.append(move(7, pool_ref.at[right], right, half1, left))
    started.append(move(8, pool_ref.at[right], right, half1, sibling))
    started[2].wait_recv()
    started.append(move(9, pool_ref.at[left], left, half1, sibling))
    started[3].wait_recv()
    started.append(move(10, pool_ref.at[right], right, half0, sibling))
    started[5].wait_recv()
    started.append(move(11, pool_ref.at[far], far, half0, sibling))
    started[7].wait_recv()
    started.append(move(12, pool_ref.at[far], far, half1, sibling))
    for n in (4, 6, 8, 9, 10, 11, 12):
        started[n].wait_recv()
    for copy in exchanges + started:
        copy.wait_send()
    keep.wait()


def normalize(values, gain):
    mean = jnp.mean(values, axis=-1, keepdims=True)
    centered = values - mean
    variance = jnp.mean(centered * centered, axis=-1, keepdims=True)
    return centered * lax.rsqrt(variance + 1e-05) * gain


def attend_kernel(
    slots, tq, big, small,
    pool_ref, gain1_ref, wqkv_ref, wout_ref, gain2_ref, whid_ref, wback_ref, out_ref,
    keys, vals_a, vals_b, stacked, accum, top, key_norm,
):
    loops = pool_ref.shape[0]
    width = gain1_ref.shape[1]
    head = width // HEADS
    kt = min(256, slots)
    scale = math.log2(math.e) / math.sqrt(head)
    me = lax.axis_index("loop")
    gain1, gain2 = gain1_ref[...], gain2_ref[...]

    def even_lane(shape):
        return lax.rem(iota(shape, 1) // head, 2) == 0

    def live_rows(j):
        note = pool_ref[j, pl.ds(slots, EXTRA), :].astype(F32)
        high, low = jnp.max(note[:, :128]), jnp.max(note[:, 128:])
        return (high * 128.0 + low).astype(jnp.int32)

    to_head = one_hot(iota((width, 128), 0) // head == iota((width, 128), 1))
    key_norm[...] = jnp.zeros_like(key_norm)

    def project(j, base):
        count = live_rows(j)

        def tile(t, carry):
            start = pl.multiple_of(t * kt, kt)
            x = pool_ref[j, pl.ds(start, kt), :].astype(F32)
            normed = normalize(x, gain1).astype(BF16)
            kv = jnp.dot(normed, wqkv_ref[:, width:], preferred_element_type=F32)
            k = kv[:, :width].astype(BF16)
            v = kv[:, width:]
            valid = iota((kt, width), 0) + start < count
            even = even_lane((kt, width))
            at = pl.ds(pl.multiple_of(base + start, 16), kt)
            keys[at, :] = k
            vals_a[at, :] = jnp.where(valid, jnp.where(even, v, 1.0), 0.0).astype(BF16)
            vals_b[at, :] = jnp.where(valid, jnp.where(even, 1.0, v), 0.0).astype(BF16)
            square = k.astype(F32)
            norms = jnp.dot((square * square).astype(BF16), to_head, preferred_element_type=F32)
            key_norm[...] = jnp.maximum(
                key_norm[...], jnp.max(norms.reshape(kt // 8, 8, 128), axis=0)
            )
            return carry

        lax.fori_loop(0, pl.cdiv(count, kt), tile, 0)
        return base + pl.cdiv(count, 16) * 16

    total_rows = lax.fori_loop(0, loops, project, jnp.int32(0))
    tail = pl.ds(pl.multiple_of(total_rows, 16), small)
    for ref in (keys, vals_a, vals_b):
        ref[tail, :] = jnp.zeros((small, width), BF16)
    key_top = jnp.max(key_norm[...], axis=0, keepdims=True)
    small_count = pl.cdiv(total_rows, small)
    big_count = small_count // (big // small)
    small_first = big_count * (big // small)

    out_ref[...] = jnp.zeros_like(out_ref)
    mine = live_rows(me)
    flag_lane = one_hot(iota((8, width), 1) == head)
    order = tuple(range(0, HEADS, 2)) + tuple(range(1, HEADS, 2))
    group = HEADS // 2 * tq

    def queries(i, carry):
        start = pl.multiple_of(i * tq, tq)
        x = pool_ref[me, pl.ds(start, tq), :].astype(F32)
        normed = normalize(x, gain1).astype(BF16)
        q = jnp.dot(normed, wqkv_ref[:, :width], preferred_element_type=F32).astype(BF16)
        lane_head = iota((tq, width), 1) // head
        for n, h in enumerate(order):
            stacked[n * tq : (n + 1) * tq, :] = jnp.where(lane_head == h, q, jnp.zeros_like(q))
        square = q.astype(F32)
        norms = jnp.dot((square * square).astype(BF16), to_head, preferred_element_type=F32)
        bound = jnp.max(jnp.max(norms, axis=0, keepdims=True) * key_top)
        accum[...] = jnp.zeros_like(accum)

        def scores(at, rows):
            return scale * lax.dot_general(
                stacked[rows, :], keys[at, :], (((1,), (1,)), ((), ())), preferred_element_type=F32
            )

        def plain(size, first):
            def step(j, carry):
                at = pl.ds(pl.multiple_of((first + j) * size, size), size)
                for rows, vals in (
                    (slice(0, group), vals_a),
                    (slice(group, 2 * group), vals_b),
                ):
                    weights = jnp.exp2(scores(at, rows)).astype(BF16)
                    accum[rows, :] += jnp.dot(weights, vals[at, :], preferred_element_type=F32)
                return carry

            return step

        def shifted(j, carry):
            at = pl.ds(pl.multiple_of(j * small, small), small)
            flags = lax.dot_general(
                flag_lane, vals_a[at, :], (((1,), (1,)), ((), ())), preferred_element_type=F32
            )
            live = flags[0:1, :] > 0.5
            for rows, vals in ((slice(0, group), vals_a), (slice(group, 2 * group), vals_b)):
                values = jnp.where(live, scores(at, rows), -1e30)
                old = top[rows, :]
                new = jnp.maximum(old, jnp.max(values, axis=1, keepdims=True))
                top[rows, :] = new
                factor = jnp.exp2(old - new)
                weights = jnp.exp2(values - new[:, :1]).astype(BF16)
                accum[rows, :] = accum[rows, :] * factor[:, :1] + jnp.dot(
                    weights, vals[at, :], preferred_element_type=F32
                )
            return carry

        unshifted = bound * (1.05 * scale * scale) < 4096.0

        @pl.when(unshifted)
        def _():
            lax.fori_loop(0, big_count, plain(big, 0), 0)
            lax.fori_loop(0, small_count - small_first, plain(small, small_first), 0)

        @pl.when(jnp.logical_not(unshifted))
        def _():
            top[...] = jnp.full(top.shape, -1e30, F32)
            lax.fori_loop(0, small_count, shifted, 0)

        part_a = jnp.zeros((tq, width), F32)
        part_b = jnp.zeros((tq, width), F32)
        pair = iota((tq, width), 1) // (2 * head)
        for n in range(HEADS // 2):
            part_a = jnp.where(pair == n, accum[n * tq : (n + 1) * tq, :], part_a)
            part_b = jnp.where(pair == n, accum[group + n * tq : group + (n + 1) * tq, :], part_b)
        even = even_lane((tq, width))
        numerator = jnp.where(even, part_a, part_b)
        sums = jnp.where(even, part_b, part_a)
        total = jnp.where(
            even, pltpu.roll(sums, width - head, 1), pltpu.roll(sums, head, 1)
        )
        attended = (numerator / total).astype(BF16)
        mixed = x + jnp.dot(attended, wout_ref[...], preferred_element_type=F32)
        normed2 = normalize(mixed, gain2).astype(BF16)
        inner = jnp.dot(normed2, whid_ref[...], preferred_element_type=F32)
        hidden = (0.5 * inner * (1.0 + lax.erf(inner * math.sqrt(0.5)))).astype(BF16)
        result = mixed + jnp.dot(hidden, wback_ref[...], preferred_element_type=F32)
        out_ref[pl.ds(start, tq), :] = result.astype(BF16)
        return carry

    lax.fori_loop(0, pl.cdiv(mine, tq), queries, 0)


def give_back_kernel(
    regions, loops, result_ref, rank_ref, place_ref, out_ref, outbox, inbox, send, recv
):
    rows = out_ref.shape[0]
    chunk = CAP * loops
    slots = regions * chunk
    region, loop = lax.axis_index("region"), lax.axis_index("loop")
    barrier = pltpu.get_barrier_semaphore()
    for k in range(1, regions):
        pl.semaphore_signal(
            barrier, inc=1, device_id=(lax.rem(region + k, regions), loop), device_id_type=MESH
        )

    def column(row_ref):
        size = row_ref.shape[1]
        row = jnp.broadcast_to(row_ref[0:1, :].astype(F32), (128, size))
        return row.T[:, 0:1].astype(jnp.int32)

    unpack = one_hot(column(rank_ref) == iota((slots, slots), 1))
    outbox[...] = jnp.dot(unpack, result_ref[...], preferred_element_type=F32).astype(BF16)
    pl.semaphore_wait(barrier, regions - 1)

    def exchange(k):
        peer = lax.rem(region + k, regions)
        return pltpu.make_async_remote_copy(
            src_ref=outbox.at[pl.ds(pl.multiple_of(peer * chunk, chunk), chunk)],
            dst_ref=inbox.at[pl.ds(pl.multiple_of(region * chunk, chunk), chunk)],
            send_sem=send.at[k],
            recv_sem=recv.at[k],
            device_id=(peer, loop),
            device_id_type=MESH,
        )

    exchanges = [exchange(k) for k in range(1, regions)]
    for copy in exchanges:
        copy.start()
    own = pl.ds(pl.multiple_of(region * chunk, chunk), chunk)
    inbox[own, :] = outbox[own, :]
    take = one_hot(column(place_ref) == iota((rows, slots), 1))
    for copy in exchanges:
        copy.wait_recv()
    out_ref[...] = jnp.dot(take, inbox[...], preferred_element_type=F32).astype(BF16)
    for copy in exchanges:
        copy.wait_send()


def local(tq, big, small, tokens, dest, norm1_gain, w_qkv, w_out, norm2_gain, w_hidden, w_back):
    rows, width = tokens.shape
    regions, loops = lax.axis_size("region"), lax.axis_size("loop")
    chunk = CAP * loops
    slots = regions * chunk
    vmem = pl.BlockSpec(memory_space=pltpu.VMEM)
    params = functools.partial(pltpu.CompilerParams, vmem_limit_bytes=48 * 1024 * 1024)
    pool, place, rank = pl.pallas_call(
        functools.partial(route_kernel, regions, loops),
        out_shape=(
            jax.ShapeDtypeStruct((loops, slots + EXTRA, width), BF16),
            jax.ShapeDtypeStruct((8, rows), jnp.int32),
            jax.ShapeDtypeStruct((8, slots), jnp.int32),
        ),
        in_specs=[vmem] * 2,
        out_specs=(pl.BlockSpec(memory_space=pl.ANY), vmem, vmem),
        scratch_shapes=[
            pltpu.VMEM((slots, width), BF16),
            pltpu.VMEM((slots, width), BF16),
            pltpu.VMEM((slots + EXTRA, width), BF16),
            pltpu.SemaphoreType.DMA((regions,)),
            pltpu.SemaphoreType.DMA((regions,)),
            pltpu.SemaphoreType.DMA((13,)),
            pltpu.SemaphoreType.DMA((13,)),
            pltpu.SemaphoreType.DMA,
        ],
        compiler_params=params(collective_id=0, has_side_effects=True),
        name="route",
    )(tokens, dest.reshape(1, rows))
    key_rows = loops * slots + small + min(256, slots)
    result = pl.pallas_call(
        functools.partial(attend_kernel, slots, tq, big, small),
        out_shape=jax.ShapeDtypeStruct((slots, width), BF16),
        in_specs=[vmem] * 7,
        out_specs=vmem,
        scratch_shapes=[
            pltpu.VMEM((key_rows, width), BF16),
            pltpu.VMEM((key_rows, width), BF16),
            pltpu.VMEM((key_rows, width), BF16),
            pltpu.VMEM((HEADS * tq, width), BF16),
            pltpu.VMEM((HEADS * tq, width), F32),
            pltpu.VMEM((HEADS * tq, 128), F32),
            pltpu.VMEM((8, 128), F32),
        ],
        compiler_params=params(),
        name="attend",
    )(
        pool, norm1_gain.reshape(1, width), w_qkv, w_out, norm2_gain.reshape(1, width),
        w_hidden, w_back,
    )
    return pl.pallas_call(
        functools.partial(give_back_kernel, regions, loops),
        out_shape=jax.ShapeDtypeStruct((rows, width), BF16),
        in_specs=[vmem] * 3,
        out_specs=vmem,
        scratch_shapes=[
            pltpu.VMEM((slots, width), BF16),
            pltpu.VMEM((slots, width), BF16),
            pltpu.SemaphoreType.DMA((regions,)),
            pltpu.SemaphoreType.DMA((regions,)),
        ],
        compiler_params=params(collective_id=1, has_side_effects=True),
        name="give_back",
    )(result, rank, place)


def build(mesh, tq, big, small):
    spread = P(("region", "loop"), None)
    return jax.shard_map(
        functools.partial(local, tq, big, small),
        mesh=mesh,
        in_specs=(spread, spread) + (P(),) * 6,
        out_specs=spread,
        check_vma=False,
    )


def solution(mesh):
    return build(mesh, 256, 2048, 512)
```

```python
import functools
import math

import jax
import jax.numpy as jnp
from jax import lax
from jax.experimental import pallas as pl
from jax.experimental.pallas import tpu as pltpu
from jax.sharding import PartitionSpec as P

HEADS = 8
CAP = 8
MARK = 16.0
MESH = pl.DeviceIdType.MESH
EXTRA = 16
F32 = jnp.float32
BF16 = jnp.bfloat16


def iota(shape, dim):
    return lax.broadcasted_iota(jnp.int32, shape, dim)


def one_hot(condition):
    return jnp.where(condition, 1.0, 0.0).astype(BF16)


def normalize(values, gain):
    mean = jnp.mean(values, axis=-1, keepdims=True)
    centered = values - mean
    variance = jnp.mean(centered * centered, axis=-1, keepdims=True)
    return centered * lax.rsqrt(variance + 1e-05) * gain


def route_kernel(
    regions, loops, tokens_ref, dest_ref, gain1_ref, pool_ref, raw_ref, place_ref, rank_ref,
    outbox, inbox, normed, packed, send_a, recv_a, send_g, recv_g, local_sem,
):
    rows, width = tokens_ref.shape
    chunk = CAP * loops
    slots = regions * chunk
    chips = loops // 2
    region, loop = lax.axis_index("region"), lax.axis_index("loop")
    chip, core = loop // 2, lax.rem(loop, 2)
    sibling = chip * 2 + (1 - core)
    right = lax.rem(chip + 1, chips) * 2 + core
    left = lax.rem(chip + chips - 1, chips) * 2 + core
    far = lax.rem(chip + 2, chips) * 2 + core

    barrier = pltpu.get_barrier_semaphore()
    for k in range(1, regions):
        pl.semaphore_signal(
            barrier, inc=1, device_id=(lax.rem(region + k, regions), loop), device_id_type=MESH
        )
    for peer in (sibling, left, right):
        pl.semaphore_signal(barrier, inc=1, device_id=(region, peer), device_id_type=MESH)

    owner_region = dest_ref[...] // loops
    hot = one_hot(owner_region == iota((regions, rows), 0))
    upper = one_hot(iota((rows, rows), 0) <= iota((rows, rows), 1))
    before = jnp.dot(hot, upper, preferred_element_type=F32)
    rank = jnp.sum(before * hot.astype(F32), axis=0, keepdims=True).astype(jnp.int32) - 1
    place = owner_region * chunk + rank
    place_ref[...] = jnp.broadcast_to(place, place_ref.shape)
    spread = one_hot(iota((slots, rows), 0) == place)
    sorted_rows = jnp.dot(spread, tokens_ref[...], preferred_element_type=F32)
    held = jnp.dot(spread, jnp.ones((rows, width), BF16), preferred_element_type=F32)
    outbox[...] = (sorted_rows + (1.0 - held) * MARK).astype(BF16)

    pl.semaphore_wait(barrier, regions - 1 + 3)

    def exchange(k):
        peer = lax.rem(region + k, regions)
        return pltpu.make_async_remote_copy(
            src_ref=outbox.at[pl.ds(pl.multiple_of(peer * chunk, chunk), chunk)],
            dst_ref=inbox.at[pl.ds(pl.multiple_of(region * chunk, chunk), chunk)],
            send_sem=send_a.at[k],
            recv_sem=recv_a.at[k],
            device_id=(peer, loop),
            device_id_type=MESH,
        )

    exchanges = [exchange(k) for k in range(1, regions)]
    for copy in exchanges:
        copy.start()
    own = pl.ds(pl.multiple_of(region * chunk, chunk), chunk)
    inbox[own, :] = outbox[own, :]
    earlier = one_hot(iota((slots, slots), 0) < iota((slots, slots), 1))

    def norm_rows(at):
        normed[at, :] = normalize(inbox[at, :].astype(F32), gain1_ref[...]).astype(BF16)

    norm_rows(own)
    for k, copy in zip(range(1, regions), exchanges):
        copy.wait_recv()
        source = lax.rem(region + regions - k, regions)
        norm_rows(pl.ds(pl.multiple_of(source * chunk, chunk), chunk))

    alive = jnp.where(inbox[:, :128].astype(F32) < 8.0, 1.0, 0.0)
    alive_row = alive.T[:16, :]
    ahead = jnp.dot(alive_row.astype(BF16), earlier, preferred_element_type=F32)
    slot = jnp.where(alive_row > 0.0, ahead, -1.0).astype(jnp.int32)
    rank_ref[...] = slot[:8, :]
    squeeze = one_hot(iota((slots, slots), 0) == slot[0:1, :])
    packed[pl.ds(0, slots), :] = jnp.dot(
        squeeze, normed[...], preferred_element_type=F32
    ).astype(BF16)
    count = jnp.sum(alive_row, axis=1, keepdims=True)
    high = jnp.floor(count * (1.0 / 128.0))
    packed[pl.ds(slots, EXTRA), :] = jnp.where(
        iota((EXTRA, width), 1) < 128, high, count - 128.0 * high
    ).astype(BF16)

    half0, half1 = pl.ds(0, slots // 2), pl.ds(slots // 2, slots // 2 + EXTRA)
    whole = pl.ds(0, slots + EXTRA)

    def move(n, src, slot_index, part, peer):
        copy = pltpu.make_async_remote_copy(
            src_ref=src.at[part],
            dst_ref=pool_ref.at[slot_index, part],
            send_sem=send_g.at[n],
            recv_sem=recv_g.at[n],
            device_id=(region, peer),
            device_id_type=MESH,
        )
        copy.start()
        return copy

    started = [
        move(0, packed, loop, half0, right),
        move(1, packed, loop, half1, left),
        move(2, packed, loop, half1, right),
        move(3, packed, loop, half0, left),
        move(4, packed, loop, whole, sibling),
    ]
    keep = pltpu.make_async_copy(packed, pool_ref.at[loop], local_sem)
    keep.start()
    raw_ref[...] = jnp.dot(squeeze, inbox[...], preferred_element_type=F32).astype(BF16)
    started[0].wait_recv()
    started.append(move(5, pool_ref.at[left], left, half0, right))
    started.append(move(6, pool_ref.at[left], left, half0, sibling))
    started[1].wait_recv()
    started.append(move(7, pool_ref.at[right], right, half1, left))
    started.append(move(8, pool_ref.at[right], right, half1, sibling))
    started[2].wait_recv()
    started.append(move(9, pool_ref.at[left], left, half1, sibling))
    started[3].wait_recv()
    started.append(move(10, pool_ref.at[right], right, half0, sibling))
    started[5].wait_recv()
    started.append(move(11, pool_ref.at[far], far, half0, sibling))
    started[7].wait_recv()
    started.append(move(12, pool_ref.at[far], far, half1, sibling))
    for n in (4, 6, 8, 9, 10, 11, 12):
        started[n].wait_recv()
    for copy in exchanges + started:
        copy.wait_send()
    keep.wait()


def attend_kernel(
    slots, tq, tail_tq, big, small,
    pool_ref, raw_ref, wqkv_hbm, wout_hbm, gain2_ref, whid_hbm, wback_hbm, out_ref,
    pool, raw, wqkv_ref, wout_ref, whid_ref, wback_ref,
    keys, vals_a, vals_b, stacked, accum, top, key_top, sems,
):
    loops, width = pool_ref.shape[0], pool_ref.shape[2]
    head = width // HEADS
    kt = min(256, slots)
    scale = math.log2(math.e) / math.sqrt(head)
    me = lax.axis_index("loop")

    loads = [
        pltpu.make_async_copy(src, dst, sems.at[n])
        for n, (src, dst) in enumerate(
            [(wqkv_hbm, wqkv_ref)]
            + [(pool_ref.at[j], pool.at[j]) for j in range(loops)]
            + [(raw_ref, raw), (wout_hbm, wout_ref), (whid_hbm, whid_ref), (wback_hbm, wback_ref)]
        )
    ]
    for load in loads:
        load.start()
    out_ref[...] = jnp.zeros_like(out_ref)
    key_top[...] = jnp.zeros_like(key_top)
    loads[0].wait()

    def even_lane(shape):
        return lax.rem(iota(shape, 1) // head, 2) == 0

    def live_rows(j):
        note = pool[j, pl.ds(slots, EXTRA), :].astype(F32)
        high, low = jnp.max(note[:, :128]), jnp.max(note[:, 128:])
        return (high * 128.0 + low).astype(jnp.int32)

    base = jnp.int32(0)
    even = even_lane((kt, width))
    for j in range(loops):
        loads[1 + j].wait()
        count = live_rows(j)

        def tile(t, carry, j=j, base=base, count=count):
            start = pl.multiple_of(t * kt, kt)
            kv = jnp.dot(
                pool[j, pl.ds(start, kt), :], wqkv_ref[:, width:], preferred_element_type=F32
            )
            k = kv[:, :width]
            v = kv[:, width:]
            valid = iota((kt, width), 0) + start < count
            at = pl.ds(pl.multiple_of(base + start, 16), kt)
            keys[at, :] = k.astype(BF16)
            vals_a[at, :] = jnp.where(valid, jnp.where(even, v, 1.0), 0.0).astype(BF16)
            vals_b[at, :] = jnp.where(valid, jnp.where(even, 1.0, v), 0.0).astype(BF16)
            peak = jnp.max(jnp.abs(k).reshape(kt // 8, 8, width), axis=0)
            key_top[...] = jnp.maximum(key_top[...], peak)
            return carry

        lax.fori_loop(0, pl.cdiv(count, kt), tile, 0)
        base = base + pl.cdiv(count, 16) * 16

    total_rows = base
    tail = pl.ds(pl.multiple_of(total_rows, 16), small)
    for ref in (keys, vals_a, vals_b):
        ref[tail, :] = jnp.zeros((small, width), BF16)
    highest = jnp.max(key_top[...], axis=0, keepdims=True)
    small_count = pl.cdiv(total_rows, small)
    big_count = small_count // (big // small)
    small_first = big_count * (big // small)
    for load in loads[1 + loops :]:
        load.wait()

    mine = live_rows(me)
    to_head = one_hot(iota((width, 128), 0) // head == iota((width, 128), 1))
    flag_lane = one_hot(iota((8, width), 1) == head)
    order = tuple(range(0, HEADS, 2)) + tuple(range(1, HEADS, 2))

    def queries(tq, start):
        group = HEADS // 2 * tq
        at_q = pl.ds(start, tq)
        q = jnp.dot(
            pool[me, at_q, :], wqkv_ref[:, :width], preferred_element_type=F32
        ).astype(BF16)
        lane_head = iota((tq, width), 1) // head
        for n, h in enumerate(order):
            stacked[n * tq : (n + 1) * tq, :] = jnp.where(lane_head == h, q, jnp.zeros_like(q))
        reach = (jnp.abs(q.astype(F32)) * highest).astype(BF16)
        bound = jnp.max(jnp.dot(reach, to_head, preferred_element_type=F32))
        accum[: 2 * group, :] = jnp.zeros((2 * group, width), F32)
        halves = ((slice(0, group), vals_a), (slice(group, 2 * group), vals_b))

        def scores(at, rows):
            return scale * lax.dot_general(
                stacked[rows, :], keys[at, :], (((1,), (1,)), ((), ())), preferred_element_type=F32
            )

        def plain(size, first):
            def step(j, carry):
                at = pl.ds(pl.multiple_of((first + j) * size, size), size)
                for rows, vals in halves:
                    weights = jnp.exp2(scores(at, rows)).astype(BF16)
                    accum[rows, :] += jnp.dot(weights, vals[at, :], preferred_element_type=F32)
                return carry

            return step

        def shifted(j, carry):
            at = pl.ds(pl.multiple_of(j * small, small), small)
            flags = lax.dot_general(
                flag_lane, vals_a[at, :], (((1,), (1,)), ((), ())), preferred_element_type=F32
            )
            live = flags[0:1, :] > 0.5
            for rows, vals in halves:
                values = jnp.where(live, scores(at, rows), -1e30)
                old = top[rows, :]
                new = jnp.maximum(old, jnp.max(values, axis=1, keepdims=True))
                top[rows, :] = new
                factor = jnp.exp2(old - new)
                weights = jnp.exp2(values - new[:, :1]).astype(BF16)
                accum[rows, :] = accum[rows, :] * factor[:, :1] + jnp.dot(
                    weights, vals[at, :], preferred_element_type=F32
                )
            return carry

        unshifted = bound * (1.02 * scale) < 90.0

        @pl.when(unshifted)
        def _():
            lax.fori_loop(0, big_count, plain(big, 0), 0)
            lax.fori_loop(0, small_count - small_first, plain(small, small_first), 0)

        @pl.when(jnp.logical_not(unshifted))
        def _():
            top[: 2 * group, :] = jnp.full((2 * group, 128), -1e30, F32)
            lax.fori_loop(0, small_count, shifted, 0)

        part_a = jnp.zeros((tq, width), F32)
        part_b = jnp.zeros((tq, width), F32)
        pair = iota((tq, width), 1) // (2 * head)
        for n in range(HEADS // 2):
            part_a = jnp.where(pair == n, accum[n * tq : (n + 1) * tq, :], part_a)
            part_b = jnp.where(pair == n, accum[group + n * tq : group + (n + 1) * tq, :], part_b)
        even = even_lane((tq, width))
        numerator = jnp.where(even, part_a, part_b)
        sums = jnp.where(even, part_b, part_a)
        total = jnp.where(
            even, pltpu.roll(sums, width - head, 1), pltpu.roll(sums, head, 1)
        )
        attended = (numerator / total).astype(BF16)
        mixed = raw[at_q, :].astype(F32) + jnp.dot(
            attended, wout_ref[...], preferred_element_type=F32
        )
        normed2 = normalize(mixed, gain2_ref[...]).astype(BF16)
        inner = jnp.dot(normed2, whid_ref[...], preferred_element_type=F32)
        hidden = (0.5 * inner * (1.0 + lax.erf(inner * math.sqrt(0.5)))).astype(BF16)
        result = mixed + jnp.dot(hidden, wback_ref[...], preferred_element_type=F32)
        out_ref[at_q, :] = result.astype(BF16)

    parts = pl.cdiv(mine, tail_tq)
    per_tile = tq // tail_tq
    full = parts // per_tile

    def full_tile(i, carry):
        queries(tq, pl.multiple_of(i * tq, tq))
        return carry

    lax.fori_loop(0, full, full_tile, 0)
    for rest in range(1, per_tile):

        @pl.when(parts - full * per_tile == rest)
        def _(rest=rest):
            queries(rest * tail_tq, pl.multiple_of(full * tq, tq))


def give_back_kernel(
    regions, loops, result_ref, rank_ref, place_ref, out_ref, outbox, inbox, send, recv
):
    rows = out_ref.shape[0]
    chunk = CAP * loops
    slots = regions * chunk
    region, loop = lax.axis_index("region"), lax.axis_index("loop")
    barrier = pltpu.get_barrier_semaphore()
    for k in range(1, regions):
        pl.semaphore_signal(
            barrier, inc=1, device_id=(lax.rem(region + k, regions), loop), device_id_type=MESH
        )

    def column(row_ref):
        size = row_ref.shape[1]
        row = jnp.broadcast_to(row_ref[0:1, :].astype(F32), (128, size))
        return row.T[:, 0:1].astype(jnp.int32)

    unpack = one_hot(column(rank_ref) == iota((slots, slots), 1))
    outbox[...] = jnp.dot(unpack, result_ref[...], preferred_element_type=F32).astype(BF16)
    pl.semaphore_wait(barrier, regions - 1)

    def exchange(k):
        peer = lax.rem(region + k, regions)
        return pltpu.make_async_remote_copy(
            src_ref=outbox.at[pl.ds(pl.multiple_of(peer * chunk, chunk), chunk)],
            dst_ref=inbox.at[pl.ds(pl.multiple_of(region * chunk, chunk), chunk)],
            send_sem=send.at[k],
            recv_sem=recv.at[k],
            device_id=(peer, loop),
            device_id_type=MESH,
        )

    exchanges = [exchange(k) for k in range(1, regions)]
    for copy in exchanges:
        copy.start()
    own = pl.ds(pl.multiple_of(region * chunk, chunk), chunk)
    inbox[own, :] = outbox[own, :]
    take = one_hot(column(place_ref) == iota((rows, slots), 1))
    for copy in exchanges:
        copy.wait_recv()
    out_ref[...] = jnp.dot(take, inbox[...], preferred_element_type=F32).astype(BF16)
    for copy in exchanges:
        copy.wait_send()


def local(
    tiles, tokens, dest, norm1_gain, w_qkv, w_out, norm2_gain, w_hidden, w_back
):
    tq, tail_tq, big, small = tiles
    rows, width = tokens.shape
    regions, loops = lax.axis_size("region"), lax.axis_size("loop")
    chunk = CAP * loops
    slots = regions * chunk
    vmem = pl.BlockSpec(memory_space=pltpu.VMEM)
    hbm = pl.BlockSpec(memory_space=pltpu.HBM)
    params = functools.partial(pltpu.CompilerParams, vmem_limit_bytes=62 * 1024 * 1024)
    pool, raw, place, rank = pl.pallas_call(
        functools.partial(route_kernel, regions, loops),
        out_shape=(
            jax.ShapeDtypeStruct((loops, slots + EXTRA, width), BF16),
            jax.ShapeDtypeStruct((slots, width), BF16),
            jax.ShapeDtypeStruct((8, rows), jnp.int32),
            jax.ShapeDtypeStruct((8, slots), jnp.int32),
        ),
        in_specs=[vmem] * 3,
        out_specs=(hbm, vmem, vmem, vmem),
        scratch_shapes=[
            pltpu.VMEM((slots, width), BF16),
            pltpu.VMEM((slots, width), BF16),
            pltpu.VMEM((slots, width), BF16),
            pltpu.VMEM((slots + EXTRA, width), BF16),
            pltpu.SemaphoreType.DMA((regions,)),
            pltpu.SemaphoreType.DMA((regions,)),
            pltpu.SemaphoreType.DMA((13,)),
            pltpu.SemaphoreType.DMA((13,)),
            pltpu.SemaphoreType.DMA,
        ],
        compiler_params=params(collective_id=0, has_side_effects=True),
        name="route",
    )(tokens, dest.reshape(1, rows), norm1_gain.reshape(1, width))
    key_rows = loops * slots + small + min(256, slots)
    result = pl.pallas_call(
        functools.partial(attend_kernel, slots, *tiles),
        out_shape=jax.ShapeDtypeStruct((slots, width), BF16),
        in_specs=[hbm, hbm, hbm, hbm, vmem, hbm, hbm],
        out_specs=vmem,
        scratch_shapes=[
            pltpu.VMEM((loops, slots + EXTRA, width), BF16),
            pltpu.VMEM((slots, width), BF16),
            pltpu.VMEM(w_qkv.shape, BF16),
            pltpu.VMEM(w_out.shape, BF16),
            pltpu.VMEM(w_hidden.shape, BF16),
            pltpu.VMEM(w_back.shape, BF16),
            pltpu.VMEM((key_rows, width), BF16),
            pltpu.VMEM((key_rows, width), BF16),
            pltpu.VMEM((key_rows, width), BF16),
            pltpu.VMEM((HEADS * tq, width), BF16),
            pltpu.VMEM((HEADS * tq, width), F32),
            pltpu.VMEM((HEADS * tq, 128), F32),
            pltpu.VMEM((8, width), F32),
            pltpu.SemaphoreType.DMA((loops + 5,)),
        ],
        compiler_params=params(),
        name="attend",
    )(pool, raw, w_qkv, w_out, norm2_gain.reshape(1, width), w_hidden, w_back)
    return pl.pallas_call(
        functools.partial(give_back_kernel, regions, loops),
        out_shape=jax.ShapeDtypeStruct((rows, width), BF16),
        in_specs=[vmem] * 3,
        out_specs=vmem,
        scratch_shapes=[
            pltpu.VMEM((slots, width), BF16),
            pltpu.VMEM((slots, width), BF16),
            pltpu.SemaphoreType.DMA((regions,)),
            pltpu.SemaphoreType.DMA((regions,)),
        ],
        compiler_params=params(collective_id=1, has_side_effects=True),
        name="give_back",
    )(result, rank, place)


def build(mesh, tiles):
    spread = P(("region", "loop"), None)
    return jax.shard_map(
        functools.partial(local, tiles),
        mesh=mesh,
        in_specs=(spread, spread) + (P(),) * 6,
        out_specs=spread,
        check_vma=False,
    )


def solution(mesh):
    return build(mesh, (256, 128, 2048, 512))
```

```python
import functools
import math

import jax
import jax.numpy as jnp
from jax import lax
from jax.experimental import pallas as pl
from jax.experimental.pallas import tpu as pltpu
from jax.sharding import PartitionSpec as P

HEADS = 8
CAP = 8
MARK = 16.0
MESH = pl.DeviceIdType.MESH
EXTRA = 16
F32 = jnp.float32
BF16 = jnp.bfloat16


def iota(shape, dim):
    return lax.broadcasted_iota(jnp.int32, shape, dim)


def one_hot(condition):
    return jnp.where(condition, 1.0, 0.0).astype(BF16)


def normalize(values, gain):
    mean = jnp.mean(values, axis=-1, keepdims=True)
    centered = values - mean
    variance = jnp.mean(centered * centered, axis=-1, keepdims=True)
    return centered * lax.rsqrt(variance + 1e-05) * gain


def head_order():
    return tuple(range(0, HEADS, 2)) + tuple(range(1, HEADS, 2))


def even_lane(shape, head):
    return lax.rem(iota(shape, 1) // head, 2) == 0


def project(rows, w_kv, valid, width):
    kv = jnp.dot(rows, w_kv, preferred_element_type=F32)
    k, v = kv[:, :width], kv[:, width:]
    even = even_lane(v.shape, width // HEADS)
    with_odd = jnp.where(valid, jnp.where(even, v, 1.0), 0.0).astype(BF16)
    with_even = jnp.where(valid, jnp.where(even, 1.0, v), 0.0).astype(BF16)
    peak = jnp.max(jnp.abs(k).reshape(k.shape[0] // 8, 8, width), axis=0)
    return k.astype(BF16), with_odd, with_even, peak


def collect(block, tq, width):
    group = HEADS // 2 * tq
    pair = iota((tq, width), 1) // (2 * (width // HEADS))
    part_a = jnp.zeros((tq, width), F32)
    part_b = jnp.zeros((tq, width), F32)
    for n in range(HEADS // 2):
        part_a = jnp.where(pair == n, block[n * tq : (n + 1) * tq, :], part_a)
        part_b = jnp.where(pair == n, block[group + n * tq : group + (n + 1) * tq, :], part_b)
    even = even_lane((tq, width), width // HEADS)
    return jnp.where(even, part_a, part_b), jnp.where(even, part_b, part_a)


def route_kernel(
    regions, loops, tq, tokens_ref, dest_ref, gain1_ref, wqkv_ref,
    late_ref, first_keys, first_a, first_b, query_ref, raw_ref, note_ref, num_ref, sum_ref,
    key_top, place_ref, rank_ref,
    outbox, inbox, normed, pool, own_late, keys, vals, stacked, accum,
    send_a, recv_a, send_g, recv_g, local_sem,
):
    rows, width = tokens_ref.shape
    chunk = CAP * loops
    slots = regions * chunk
    half = slots // 2
    chips = loops // 2
    head = width // HEADS
    scale = math.log2(math.e) / math.sqrt(head)
    region, loop = lax.axis_index("region"), lax.axis_index("loop")
    chip, core = loop // 2, lax.rem(loop, 2)
    sibling = chip * 2 + (1 - core)
    right_chip, left_chip = lax.rem(chip + 1, chips), lax.rem(chip + chips - 1, chips)
    far_chip = lax.rem(chip + 2, chips)
    right, left, far = right_chip * 2 + core, left_chip * 2 + core, far_chip * 2 + core

    barrier = pltpu.get_barrier_semaphore()
    for k in range(1, regions):
        pl.semaphore_signal(
            barrier, inc=1, device_id=(lax.rem(region + k, regions), loop), device_id_type=MESH
        )
    for peer in (sibling, left, right):
        pl.semaphore_signal(barrier, inc=1, device_id=(region, peer), device_id_type=MESH)

    owner_region = dest_ref[...] // loops
    hot = one_hot(owner_region == iota((regions, rows), 0))
    upper = one_hot(iota((rows, rows), 0) <= iota((rows, rows), 1))
    before = jnp.dot(hot, upper, preferred_element_type=F32)
    rank = jnp.sum(before * hot.astype(F32), axis=0, keepdims=True).astype(jnp.int32) - 1
    place = owner_region * chunk + rank
    place_ref[...] = jnp.broadcast_to(place, place_ref.shape)
    spread = one_hot(iota((slots, rows), 0) == place)
    sorted_rows = jnp.dot(spread, tokens_ref[...], preferred_element_type=F32)
    held = jnp.dot(spread, jnp.ones((rows, width), BF16), preferred_element_type=F32)
    outbox[...] = (sorted_rows + (1.0 - held) * MARK).astype(BF16)

    pl.semaphore_wait(barrier, regions - 1 + 3)

    def exchange(k):
        peer = lax.rem(region + k, regions)
        return pltpu.make_async_remote_copy(
            src_ref=outbox.at[pl.ds(pl.multiple_of(peer * chunk, chunk), chunk)],
            dst_ref=inbox.at[pl.ds(pl.multiple_of(region * chunk, chunk), chunk)],
            send_sem=send_a.at[k],
            recv_sem=recv_a.at[k],
            device_id=(peer, loop),
            device_id_type=MESH,
        )

    exchanges = [exchange(k) for k in range(1, regions)]
    for copy in exchanges:
        copy.start()
    own = pl.ds(pl.multiple_of(region * chunk, chunk), chunk)
    inbox[own, :] = outbox[own, :]
    earlier = one_hot(iota((slots, slots), 0) < iota((slots, slots), 1))

    def norm_rows(at):
        normed[at, :] = normalize(inbox[at, :].astype(F32), gain1_ref[...]).astype(BF16)

    norm_rows(own)
    for k, copy in zip(range(1, regions), exchanges):
        copy.wait_recv()
        source = lax.rem(region + regions - k, regions)
        norm_rows(pl.ds(pl.multiple_of(source * chunk, chunk), chunk))

    alive = jnp.where(inbox[:, :128].astype(F32) < 8.0, 1.0, 0.0)
    alive_row = alive.T[:16, :]
    ahead = jnp.dot(alive_row.astype(BF16), earlier, preferred_element_type=F32)
    slot = jnp.where(alive_row > 0.0, ahead, -1.0).astype(jnp.int32)
    rank_ref[...] = slot[:8, :]
    squeeze = one_hot(iota((slots, slots), 0) == slot[0:1, :])
    packed = jnp.dot(squeeze, normed[...], preferred_element_type=F32).astype(BF16)
    count = jnp.sum(alive_row, axis=1, keepdims=True)
    high = jnp.floor(count * (1.0 / 128.0))
    pool[loop, pl.ds(0, EXTRA), :] = jnp.where(
        iota((EXTRA, width), 1) < 128, high, count - 128.0 * high
    ).astype(BF16)
    pool[loop, pl.ds(EXTRA, half), :] = packed[:half, :]
    own_late[...] = packed[half:, :]

    def move(n, src, dst, peer):
        return pltpu.make_async_remote_copy(
            src_ref=src,
            dst_ref=dst,
            send_sem=send_g.at[n],
            recv_sem=recv_g.at[n],
            device_id=(region, peer),
            device_id_type=MESH,
        )

    def early(n, index, peer):
        return move(n, pool.at[index], pool.at[index], peer)

    def late(n, index, peer):
        return move(n, late_ref.at[index], late_ref.at[index], peer)

    moves = [
        early(0, loop, right),
        early(1, loop, left),
        early(2, loop, sibling),
        move(3, own_late, late_ref.at[loop], right),
        move(4, own_late, late_ref.at[loop], left),
        move(5, own_late, late_ref.at[loop], sibling),
        early(6, left, right),
        early(7, left, sibling),
        early(8, right, sibling),
        late(9, right, left),
        late(10, right, sibling),
        late(11, left, sibling),
        early(12, far, sibling),
        late(13, far, sibling),
    ]
    for n in range(6):
        moves[n].start()
    keep = pltpu.make_async_copy(own_late, late_ref.at[loop], local_sem.at[0])
    keep.start()

    own_rows = jnp.concatenate([pool[loop, pl.ds(EXTRA, half), :], own_late[...]], axis=0)
    q_all = jnp.dot(own_rows, wqkv_ref[:, :width], preferred_element_type=F32).astype(BF16)
    query_ref[...] = q_all
    tiles = half // tq
    lane_head = iota((tq, width), 1) // head
    for t in range(tiles):
        q = q_all[t * tq : (t + 1) * tq, :]
        for n, h in enumerate(head_order()):
            stacked[t, n * tq : (n + 1) * tq, :] = jnp.where(lane_head == h, q, jnp.zeros_like(q))
    raw_ref[...] = jnp.dot(squeeze, inbox[...], preferred_element_type=F32).astype(BF16)
    accum[...] = jnp.zeros_like(accum)
    key_top[...] = jnp.zeros_like(key_top)

    group = HEADS // 2 * tq

    def hand_over(p):
        at = pl.ds(pl.multiple_of(2 * p * half, 2 * half), 2 * half)
        return [
            pltpu.make_async_copy(src.at[at], dst.at[at], local_sem.at[1 + 3 * p + n])
            for n, (src, dst) in enumerate(
                ((keys, first_keys), (vals.at[0], first_a), (vals.at[1], first_b))
            )
        ]

    def prepare(p):
        turn = jnp.where(p == 1, chips - 1, jnp.where(p == 2, 1, jnp.where(p == 3, 2, 0)))

        def one(c, carry):
            j = lax.rem(chip + turn, chips) * 2 + lax.rem(core + c, 2)
            note = pool[j, pl.ds(0, EXTRA), :]
            note_ref[j] = note
            note = note.astype(F32)
            live = note[0:1, 0:1] * 128.0 + note[0:1, 128:129]
            valid = iota((half, width), 0).astype(F32) < live
            k, va, vb, peak = project(
                pool[j, pl.ds(EXTRA, half), :], wqkv_ref[:, width:], valid, width
            )
            at = pl.ds(pl.multiple_of((2 * p + c) * half, half), half)
            keys[at, :] = k
            vals[0, at, :] = va
            vals[1, at, :] = vb
            key_top[...] = jnp.maximum(key_top[...], peak)
            return carry

        lax.fori_loop(0, 2, one, 0)
        for copy in hand_over(p):
            copy.start()

    script = {
        0: ["w2"],
        tiles: ["w0", "s6", "s7", "w1", "s8", "w7"],
        tiles + tiles // 2: ["w4", "s9", "s10", "w3", "s11"],
        2 * tiles: ["w8"],
        3 * tiles: ["w6", "s12", "w9", "s13", "w12"],
    }

    def advance(step, carry):
        p, tile = step // tiles, lax.rem(step, tiles)
        for when, acts in script.items():

            @pl.when(step == when)
            def _(acts=acts):
                for act in acts:
                    copy = moves[int(act[1:])]
                    if act[0] == "w":
                        copy.wait_recv()
                    else:
                        copy.start()

        @pl.when(tile == 0)
        def _():
            prepare(p)

        at = pl.ds(pl.multiple_of(2 * p * half, 2 * half), 2 * half)

        def part(side, carry):
            lines = pl.ds(pl.multiple_of(side * group, group), group)
            scores = scale * lax.dot_general(
                stacked[tile, lines, :], keys[at, :], (((1,), (1,)), ((), ())),
                preferred_element_type=F32,
            )
            weights = jnp.exp2(scores).astype(BF16)
            accum[tile, lines, :] += jnp.dot(
                weights, vals[side, at, :], preferred_element_type=F32
            )
            return carry

        return lax.fori_loop(0, 2, part, carry)

    lax.fori_loop(0, 4 * tiles, advance, 0)
    for t in range(tiles):
        numerator, sums = collect(accum[t], tq, width)
        num_ref[t * tq : (t + 1) * tq, :] = numerator
        sum_ref[t * tq : (t + 1) * tq, :] = sums
    for n in (5, 10, 11, 13):
        moves[n].wait_recv()
    for copy in exchanges + moves:
        copy.wait_send()
    keep.wait()
    for p in range(4):
        for copy in hand_over(p):
            copy.wait()


def attend_kernel(
    tq, big, small,
    late_hbm, first_keys, first_a, first_b, query_hbm, raw_hbm, num_hbm, sum_hbm, wqkv_hbm,
    wout_hbm, whid_hbm, wback_hbm, note_ref, first_top, gain2_ref, out_ref,
    late, query, raw, num, sums_in, wkv, wout, whid, wback,
    keys, vals_a, vals_b, stacked, accum, top, key_top, sems,
):
    loops, half, width = late_hbm.shape
    slots = query_hbm.shape[0]
    head = width // HEADS
    kt = min(256, half)
    early_rows = loops * half
    scale = math.log2(math.e) / math.sqrt(head)
    me = lax.axis_index("loop")

    pairs = [(wqkv_hbm.at[:, pl.ds(width, 2 * width)], wkv)]
    pairs += [(late_hbm.at[j], late.at[j]) for j in range(loops)]
    pairs += [(query_hbm, query), (raw_hbm, raw), (num_hbm, num), (sum_hbm, sums_in)]
    pairs += [(wout_hbm, wout), (whid_hbm, whid), (wback_hbm, wback)]
    front = pl.ds(0, early_rows)
    pairs += [
        (first_keys, keys.at[front]), (first_a, vals_a.at[front]), (first_b, vals_b.at[front]),
    ]
    loads = [pltpu.make_async_copy(src, dst, sems.at[n]) for n, (src, dst) in enumerate(pairs)]
    for load in loads:
        load.start()
    out_ref[...] = jnp.zeros_like(out_ref)
    key_top[...] = first_top[...]

    def live_rows(j):
        note = note_ref[j].astype(F32)
        high, low = jnp.max(note[:, :128]), jnp.max(note[:, 128:])
        return (high * 128.0 + low).astype(jnp.int32)

    counts = [live_rows(j) for j in range(loops)]
    loads[0].wait()
    base = jnp.int32(early_rows)
    for j in range(loops):
        loads[1 + j].wait()
        count = jnp.maximum(counts[j] - half, 0)

        def tile(t, carry, j=j, base=base, count=count):
            start = pl.multiple_of(t * kt, kt)
            valid = iota((kt, width), 0) + start < count
            k, va, vb, peak = project(late[j, pl.ds(start, kt), :], wkv[...], valid, width)
            at = pl.ds(pl.multiple_of(base + start, 16), kt)
            keys[at, :] = k
            vals_a[at, :] = va
            vals_b[at, :] = vb
            key_top[...] = jnp.maximum(key_top[...], peak)
            return carry

        lax.fori_loop(0, pl.cdiv(count, kt), tile, 0)
        base = base + pl.cdiv(count, 16) * 16

    total_rows = base
    tail = pl.ds(pl.multiple_of(total_rows, 16), small)
    for ref in (keys, vals_a, vals_b):
        ref[tail, :] = jnp.zeros((small, width), BF16)
    highest = jnp.max(key_top[...], axis=0, keepdims=True)
    for load in loads[1 + loops : -3]:
        load.wait()

    mine = live_rows(me)
    to_head = one_hot(iota((width, 128), 0) // head == iota((width, 128), 1))
    flag_lane = one_hot(iota((8, width), 1) == head)
    reach = (jnp.abs(query[...].astype(F32)) * highest).astype(BF16)
    bound = jnp.max(jnp.dot(reach, to_head, preferred_element_type=F32))
    unshifted = bound * (1.02 * scale) < 90.0

    def wait_early(condition):
        @pl.when(condition)
        def _():
            for load in loads[-3:]:
                load.wait()

    wait_early(jnp.logical_not(unshifted))

    def queries(tq, start):
        group = HEADS // 2 * tq
        at_q = pl.ds(start, tq)
        q = query[at_q, :]
        lane_head = iota((tq, width), 1) // head
        for n, h in enumerate(head_order()):
            stacked[n * tq : (n + 1) * tq, :] = jnp.where(lane_head == h, q, jnp.zeros_like(q))
        accum[: 2 * group, :] = jnp.zeros((2 * group, width), F32)
        halves = ((slice(0, group), vals_a), (slice(group, 2 * group), vals_b))
        begun = jnp.logical_and(unshifted, start < half)
        first = jnp.where(begun, early_rows, 0)
        blocks = pl.cdiv(total_rows - first, small)

        def scores(at, rows):
            return scale * lax.dot_general(
                stacked[rows, :], keys[at, :], (((1,), (1,)), ((), ())), preferred_element_type=F32
            )

        def plain(size, offset):
            at = pl.ds(pl.multiple_of(offset, 16), size)
            for rows, vals in halves:
                weights = jnp.exp2(scores(at, rows)).astype(BF16)
                accum[rows, :] += jnp.dot(weights, vals[at, :], preferred_element_type=F32)

        def shifted(j, carry):
            at = pl.ds(pl.multiple_of(j * small, small), small)
            flags = lax.dot_general(
                flag_lane, vals_a[at, :], (((1,), (1,)), ((), ())), preferred_element_type=F32
            )
            live = flags[0:1, :] > 0.5
            for rows, vals in halves:
                values = jnp.where(live, scores(at, rows), -1e30)
                old = top[rows, :]
                new = jnp.maximum(old, jnp.max(values, axis=1, keepdims=True))
                top[rows, :] = new
                factor = jnp.exp2(old - new)
                weights = jnp.exp2(values - new[:, :1]).astype(BF16)
                accum[rows, :] = accum[rows, :] * factor[:, :1] + jnp.dot(
                    weights, vals[at, :], preferred_element_type=F32
                )
            return carry

        @pl.when(unshifted)
        def _():
            per = big // small
            many = blocks // per

            def step(j, carry):
                plain(big, first + j * big)
                return carry

            lax.fori_loop(0, many, step, 0)
            left = blocks - many * per
            offset = first + many * big
            size = big // 2
            while size >= small:
                units = size // small
                taken = left >= units

                @pl.when(taken)
                def _(size=size, offset=offset):
                    plain(size, offset)

                left = jnp.where(taken, left - units, left)
                offset = jnp.where(taken, offset + size, offset)
                size //= 2

        @pl.when(jnp.logical_not(unshifted))
        def _():
            top[: 2 * group, :] = jnp.full((2 * group, 128), -1e30, F32)
            lax.fori_loop(0, blocks, shifted, 0)

        numerator, sums = collect(accum[: 2 * group, :], tq, width)
        at_p = pl.ds(pl.multiple_of(jnp.where(start < half, start, 0), 16), tq)
        numerator = numerator + jnp.where(begun, num[at_p, :], 0.0)
        sums = sums + jnp.where(begun, sums_in[at_p, :], 0.0)
        even = even_lane((tq, width), head)
        total = jnp.where(
            even, pltpu.roll(sums, width - head, 1), pltpu.roll(sums, head, 1)
        )
        attended = (numerator / total).astype(BF16)
        mixed = raw[at_q, :].astype(F32) + jnp.dot(
            attended, wout[...], preferred_element_type=F32
        )
        normed2 = normalize(mixed, gain2_ref[...]).astype(BF16)
        inner = jnp.dot(normed2, whid[...], preferred_element_type=F32)
        hidden = (0.5 * inner * (1.0 + lax.erf(inner * math.sqrt(0.5)))).astype(BF16)
        result = mixed + jnp.dot(hidden, wback[...], preferred_element_type=F32)
        out_ref[at_q, :] = result.astype(BF16)

    tiles = pl.cdiv(mine, tq)
    begun_tiles = half // tq

    def each_tile(i, carry):
        wait_early(jnp.logical_and(unshifted, i == begun_tiles))
        queries(tq, pl.multiple_of(i * tq, tq))
        return carry

    lax.fori_loop(0, tiles, each_tile, 0)
    wait_early(jnp.logical_and(unshifted, tiles <= begun_tiles))


def give_back_kernel(
    regions, loops, result_ref, rank_ref, place_ref, out_ref, outbox, inbox, send, recv
):
    rows = out_ref.shape[0]
    chunk = CAP * loops
    slots = regions * chunk
    region, loop = lax.axis_index("region"), lax.axis_index("loop")
    barrier = pltpu.get_barrier_semaphore()
    for k in range(1, regions):
        pl.semaphore_signal(
            barrier, inc=1, device_id=(lax.rem(region + k, regions), loop), device_id_type=MESH
        )

    def column(row_ref):
        size = row_ref.shape[1]
        row = jnp.broadcast_to(row_ref[0:1, :].astype(F32), (128, size))
        return row.T[:, 0:1].astype(jnp.int32)

    unpack = one_hot(column(rank_ref) == iota((slots, slots), 1))
    outbox[...] = jnp.dot(unpack, result_ref[...], preferred_element_type=F32).astype(BF16)
    pl.semaphore_wait(barrier, regions - 1)

    def exchange(k):
        peer = lax.rem(region + k, regions)
        return pltpu.make_async_remote_copy(
            src_ref=outbox.at[pl.ds(pl.multiple_of(peer * chunk, chunk), chunk)],
            dst_ref=inbox.at[pl.ds(pl.multiple_of(region * chunk, chunk), chunk)],
            send_sem=send.at[k],
            recv_sem=recv.at[k],
            device_id=(peer, loop),
            device_id_type=MESH,
        )

    exchanges = [exchange(k) for k in range(1, regions)]
    for copy in exchanges:
        copy.start()
    own = pl.ds(pl.multiple_of(region * chunk, chunk), chunk)
    inbox[own, :] = outbox[own, :]
    take = one_hot(column(place_ref) == iota((rows, slots), 1))
    for copy in exchanges:
        copy.wait_recv()
    out_ref[...] = jnp.dot(take, inbox[...], preferred_element_type=F32).astype(BF16)
    for copy in exchanges:
        copy.wait_send()


def local(
    tiles, tokens, dest, norm1_gain, w_qkv, w_out, norm2_gain, w_hidden, w_back
):
    tq, big, small = tiles
    rows, width = tokens.shape
    regions, loops = lax.axis_size("region"), lax.axis_size("loop")
    chunk = CAP * loops
    slots = regions * chunk
    half = slots // 2
    vmem = pl.BlockSpec(memory_space=pltpu.VMEM)
    hbm = pl.BlockSpec(memory_space=pltpu.HBM)
    params = functools.partial(pltpu.CompilerParams, vmem_limit_bytes=62 * 1024 * 1024)
    shape = jax.ShapeDtypeStruct
    (
        late, first_keys, first_a, first_b, query, raw, notes, num, sums, key_top, place, rank,
    ) = pl.pallas_call(
        functools.partial(route_kernel, regions, loops, tq),
        out_shape=(
            shape((loops, half, width), BF16),
            shape((loops * half, width), BF16),
            shape((loops * half, width), BF16),
            shape((loops * half, width), BF16),
            shape((slots, width), BF16),
            shape((slots, width), BF16),
            shape((loops, EXTRA, width), BF16),
            shape((half, width), F32),
            shape((half, width), F32),
            shape((8, width), F32),
            shape((8, rows), jnp.int32),
            shape((8, slots), jnp.int32),
        ),
        in_specs=[vmem] * 4,
        out_specs=(hbm,) * 4 + (vmem,) * 8,
        scratch_shapes=[
            pltpu.VMEM((slots, width), BF16),
            pltpu.VMEM((slots, width), BF16),
            pltpu.VMEM((slots, width), BF16),
            pltpu.VMEM((loops, half + EXTRA, width), BF16),
            pltpu.VMEM((half, width), BF16),
            pltpu.VMEM((loops * half, width), BF16),
            pltpu.VMEM((2, loops * half, width), BF16),
            pltpu.VMEM((half // tq, HEADS * tq, width), BF16),
            pltpu.VMEM((half // tq, HEADS * tq, width), F32),
            pltpu.SemaphoreType.DMA((regions,)),
            pltpu.SemaphoreType.DMA((regions,)),
            pltpu.SemaphoreType.DMA((14,)),
            pltpu.SemaphoreType.DMA((14,)),
            pltpu.SemaphoreType.DMA((13,)),
        ],
        compiler_params=params(collective_id=0, has_side_effects=True),
        name="route",
    )(tokens, dest.reshape(1, rows), norm1_gain.reshape(1, width), w_qkv)
    key_rows = loops * slots + small + min(256, half)
    result = pl.pallas_call(
        functools.partial(attend_kernel, *tiles),
        out_shape=shape((slots, width), BF16),
        in_specs=[hbm] * 12 + [vmem] * 3,
        out_specs=vmem,
        scratch_shapes=[
            pltpu.VMEM((loops, half, width), BF16),
            pltpu.VMEM((slots, width), BF16),
            pltpu.VMEM((slots, width), BF16),
            pltpu.VMEM((half, width), F32),
            pltpu.VMEM((half, width), F32),
            pltpu.VMEM((width, 2 * width), BF16),
            pltpu.VMEM(w_out.shape, BF16),
            pltpu.VMEM(w_hidden.shape, BF16),
            pltpu.VMEM(w_back.shape, BF16),
            pltpu.VMEM((key_rows, width), BF16),
            pltpu.VMEM((key_rows, width), BF16),
            pltpu.VMEM((key_rows, width), BF16),
            pltpu.VMEM((HEADS * tq, width), BF16),
            pltpu.VMEM((HEADS * tq, width), F32),
            pltpu.VMEM((HEADS * tq, 128), F32),
            pltpu.VMEM((8, width), F32),
            pltpu.SemaphoreType.DMA((loops + 11,)),
        ],
        compiler_params=params(),
        name="attend",
    )(
        late, first_keys, first_a, first_b, query, raw, num, sums, w_qkv, w_out, w_hidden,
        w_back, notes, key_top, norm2_gain.reshape(1, width),
    )
    return pl.pallas_call(
        functools.partial(give_back_kernel, regions, loops),
        out_shape=jax.ShapeDtypeStruct((rows, width), BF16),
        in_specs=[vmem] * 3,
        out_specs=vmem,
        scratch_shapes=[
            pltpu.VMEM((slots, width), BF16),
            pltpu.VMEM((slots, width), BF16),
            pltpu.SemaphoreType.DMA((regions,)),
            pltpu.SemaphoreType.DMA((regions,)),
        ],
        compiler_params=params(collective_id=1, has_side_effects=True),
        name="give_back",
    )(result, rank, place)


def build(mesh, tiles):
    spread = P(("region", "loop"), None)
    return jax.shard_map(
        functools.partial(local, tiles),
        mesh=mesh,
        in_specs=(spread, spread) + (P(),) * 6,
        out_specs=spread,
        check_vma=False,
    )


def solution(mesh):
    return build(mesh, (256, 2048, 512))
```

```python
import functools
import math

import jax
import jax.numpy as jnp
from jax import lax
from jax.experimental import pallas as pl
from jax.experimental.pallas import tpu as pltpu
from jax.sharding import PartitionSpec as P

HEADS = 8
CAP = 8
MARK = 16.0
MESH = pl.DeviceIdType.MESH
EXTRA = 16
F32 = jnp.float32
BF16 = jnp.bfloat16


def iota(shape, dim):
    return lax.broadcasted_iota(jnp.int32, shape, dim)


def one_hot(condition):
    return jnp.where(condition, 1.0, 0.0).astype(BF16)


def normalize(values, gain):
    mean = jnp.mean(values, axis=-1, keepdims=True)
    centered = values - mean
    variance = jnp.mean(centered * centered, axis=-1, keepdims=True)
    return centered * lax.rsqrt(variance + 1e-05) * gain


def head_order():
    return tuple(range(0, HEADS, 2)) + tuple(range(1, HEADS, 2))


def even_lane(shape, head):
    return lax.rem(iota(shape, 1) // head, 2) == 0


def project(rows, w_kv, valid, width):
    kv = jnp.dot(rows, w_kv, preferred_element_type=F32)
    k, v = kv[:, :width], kv[:, width:]
    even = even_lane(v.shape, width // HEADS)
    with_odd = jnp.where(valid, jnp.where(even, v, 1.0), 0.0).astype(BF16)
    with_even = jnp.where(valid, jnp.where(even, 1.0, v), 0.0).astype(BF16)
    peak = jnp.max(jnp.abs(k).reshape(k.shape[0] // 8, 8, width), axis=0)
    return k.astype(BF16), with_odd, with_even, peak


def collect(block, tq, width):
    group = HEADS // 2 * tq
    pair = iota((tq, width), 1) // (2 * (width // HEADS))
    part_a = jnp.zeros((tq, width), F32)
    part_b = jnp.zeros((tq, width), F32)
    for n in range(HEADS // 2):
        part_a = jnp.where(pair == n, block[n * tq : (n + 1) * tq, :], part_a)
        part_b = jnp.where(pair == n, block[group + n * tq : group + (n + 1) * tq, :], part_b)
    even = even_lane((tq, width), width // HEADS)
    return jnp.where(even, part_a, part_b), jnp.where(even, part_b, part_a)


def route_kernel(
    regions, loops, tq, tokens_ref, dest_ref, gain1_ref, wqkv_ref,
    late_ref, first_keys, first_a, first_b, query_ref, raw_ref, note_ref, num_ref, sum_ref,
    key_top, place_ref, rank_ref,
    outbox, inbox, query, raw, pool, own_late, keys, vals, stacked, accum,
    send_a, recv_a, send_g, recv_g, local_sem,
):
    rows, width = tokens_ref.shape
    chunk = CAP * loops
    slots = regions * chunk
    half = slots // 2
    chips = loops // 2
    head = width // HEADS
    scale = math.log2(math.e) / math.sqrt(head)
    region, loop = lax.axis_index("region"), lax.axis_index("loop")
    chip, core = loop // 2, lax.rem(loop, 2)
    sibling = chip * 2 + (1 - core)
    right_chip, left_chip = lax.rem(chip + 1, chips), lax.rem(chip + chips - 1, chips)
    far_chip = lax.rem(chip + 2, chips)
    right, left, far = right_chip * 2 + core, left_chip * 2 + core, far_chip * 2 + core

    barrier = pltpu.get_barrier_semaphore()
    for k in range(1, regions):
        pl.semaphore_signal(
            barrier, inc=1, device_id=(lax.rem(region + k, regions), loop), device_id_type=MESH
        )
    for peer in (sibling, left, right):
        pl.semaphore_signal(barrier, inc=1, device_id=(region, peer), device_id_type=MESH)

    owner_region = dest_ref[...] // loops
    hot = one_hot(owner_region == iota((regions, rows), 0))
    not_later = one_hot(iota((rows, rows), 0) <= iota((rows, rows), 1))
    before = jnp.dot(hot, not_later, preferred_element_type=F32)
    rank = jnp.sum(before * hot.astype(F32), axis=0, keepdims=True).astype(jnp.int32) - 1
    place = owner_region * chunk + rank
    place_ref[...] = jnp.broadcast_to(place, place_ref.shape)
    spread = one_hot(iota((slots, rows), 0) == place)
    sorted_rows = jnp.dot(spread, tokens_ref[...], preferred_element_type=F32)
    held = jnp.dot(spread, jnp.ones((rows, width), BF16), preferred_element_type=F32)
    outbox[...] = (sorted_rows + (1.0 - held) * MARK).astype(BF16)

    pl.semaphore_wait(barrier, regions - 1 + 3)

    def exchange(k):
        peer = lax.rem(region + k, regions)
        return pltpu.make_async_remote_copy(
            src_ref=outbox.at[pl.ds(pl.multiple_of(peer * chunk, chunk), chunk)],
            dst_ref=inbox.at[pl.ds(pl.multiple_of(region * chunk, chunk), chunk)],
            send_sem=send_a.at[k],
            recv_sem=recv_a.at[k],
            device_id=(peer, loop),
            device_id_type=MESH,
        )

    exchanges = [exchange(k) for k in range(1, regions)]
    for copy in exchanges:
        copy.start()
    own = pl.ds(pl.multiple_of(region * chunk, chunk), chunk)
    inbox[own, :] = outbox[own, :]
    earlier = one_hot(iota((slots, slots), 0) < iota((slots, slots), 1))

    for copy in exchanges:
        copy.wait_recv()
    landed = inbox[...]
    normed = normalize(landed.astype(F32), gain1_ref[...]).astype(BF16)

    alive = jnp.where(landed[:, :128].astype(F32) < 8.0, 1.0, 0.0)
    alive_row = alive.T[:16, :]
    ahead = jnp.dot(alive_row.astype(BF16), earlier, preferred_element_type=F32)
    slot = jnp.where(alive_row > 0.0, ahead, -1.0).astype(jnp.int32)
    rank_ref[...] = slot[:8, :]
    squeeze = one_hot(iota((slots, slots), 0) == slot[0:1, :])
    packed = jnp.dot(squeeze, normed, preferred_element_type=F32).astype(BF16)
    count = jnp.sum(alive_row, axis=1, keepdims=True)
    tens = jnp.floor(count * (1.0 / 128.0))
    pool[loop, pl.ds(0, EXTRA), :] = jnp.where(
        iota((EXTRA, width), 1) < 128, tens, count - 128.0 * tens
    ).astype(BF16)
    pool[loop, pl.ds(EXTRA, half), :] = packed[:half, :]
    own_late[...] = packed[half:, :]

    def move(n, src, dst, peer):
        return pltpu.make_async_remote_copy(
            src_ref=src,
            dst_ref=dst,
            send_sem=send_g.at[n],
            recv_sem=recv_g.at[n],
            device_id=(region, peer),
            device_id_type=MESH,
        )

    quarter = half // 2
    upper, lower = pl.ds(0, EXTRA + quarter), pl.ds(EXTRA + quarter, quarter)
    high, low = pl.ds(0, quarter), pl.ds(quarter, quarter)

    def early(n, index, peer, *part):
        return move(n, pool.at[(index, *part)], pool.at[(index, *part)], peer)

    def late(n, index, peer, *part):
        return move(n, late_ref.at[(index, *part)], late_ref.at[(index, *part)], peer)

    moves = [
        early(0, loop, right),
        early(1, loop, left),
        early(2, loop, sibling),
        move(3, own_late, late_ref.at[loop], right),
        move(4, own_late, late_ref.at[loop], left),
        move(5, own_late, late_ref.at[loop], sibling),
        early(6, left, right, upper),
        early(7, right, left, lower),
        early(8, left, sibling),
        early(9, right, sibling),
        early(10, far, sibling, upper),
        early(11, far, sibling, lower),
        late(12, left, right, high),
        late(13, right, left, low),
        late(14, left, sibling),
        late(15, right, sibling),
        late(16, far, sibling, high),
        late(17, far, sibling, low),
    ]
    for n in range(3):
        moves[n].start()
    keep = pltpu.make_async_copy(own_late, late_ref.at[loop], local_sem.at[0])
    keep.start()

    own_rows = jnp.concatenate([pool[loop, pl.ds(EXTRA, half), :], own_late[...]], axis=0)
    q_all = jnp.dot(own_rows, wqkv_ref[:, :width], preferred_element_type=F32).astype(BF16)
    query[...] = q_all
    tiles = half // tq
    lane_head = iota((tq, width), 1) // head
    for t in range(tiles):
        q = q_all[t * tq : (t + 1) * tq, :]
        for n, h in enumerate(head_order()):
            stacked[t, n * tq : (n + 1) * tq, :] = jnp.where(lane_head == h, q, jnp.zeros_like(q))
    raw[...] = jnp.dot(squeeze, landed, preferred_element_type=F32).astype(BF16)
    own_out = [
        pltpu.make_async_copy(query, query_ref, local_sem.at[13]),
        pltpu.make_async_copy(raw, raw_ref, local_sem.at[14]),
    ]
    for copy in own_out:
        copy.start()
    accum[...] = jnp.zeros_like(accum)
    key_top[...] = jnp.zeros_like(key_top)

    group = HEADS // 2 * tq

    def hand_over(p):
        at = pl.ds(pl.multiple_of(2 * p * half, 2 * half), 2 * half)
        return [
            pltpu.make_async_copy(src.at[at], dst.at[at], local_sem.at[1 + 3 * p + n])
            for n, (src, dst) in enumerate(
                ((keys, first_keys), (vals.at[0], first_a), (vals.at[1], first_b))
            )
        ]

    def prepare(p):
        turn = jnp.where(p == 1, chips - 1, jnp.where(p == 2, 1, jnp.where(p == 3, 2, 0)))

        def one(c, carry):
            j = lax.rem(chip + turn, chips) * 2 + lax.rem(core + c, 2)
            note = pool[j, pl.ds(0, EXTRA), :]
            note_ref[j] = note
            note = note.astype(F32)
            live = note[0:1, 0:1] * 128.0 + note[0:1, 128:129]
            valid = iota((half, width), 0).astype(F32) < live
            k, va, vb, peak = project(
                pool[j, pl.ds(EXTRA, half), :], wqkv_ref[:, width:], valid, width
            )
            at = pl.ds(pl.multiple_of((2 * p + c) * half, half), half)
            keys[at, :] = k
            vals[0, at, :] = va
            vals[1, at, :] = vb
            key_top[...] = jnp.maximum(key_top[...], peak)
            return carry

        lax.fori_loop(0, 2, one, 0)
        for copy in hand_over(p):
            copy.start()

    script = {
        0: "w2",
        1: "w0 w1 s6 s7 s8 s9 s3 s4 s5",
        tiles: "w8",
        tiles + 1: "w6 w7 s10 s11",
        2 * tiles: "w9",
        2 * tiles + 1: "w3 w4 s12 s13 s14 s15",
        3 * tiles: "w10 w11",
        3 * tiles + 1: "w12 w13 s16 s17",
    }

    def advance(step, carry):
        p, tile = step // tiles, lax.rem(step, tiles)
        for when, acts in script.items():

            @pl.when(step == when)
            def _(acts=acts):
                for act in acts.split():
                    copy = moves[int(act[1:])]
                    if act[0] == "w":
                        copy.wait_recv()
                    else:
                        copy.start()

        @pl.when(tile == 0)
        def _():
            prepare(p)

        at = pl.ds(pl.multiple_of(2 * p * half, 2 * half), 2 * half)

        def part(side, carry):
            lines = pl.ds(pl.multiple_of(side * group, group), group)
            scores = scale * lax.dot_general(
                stacked[tile, lines, :], keys[at, :], (((1,), (1,)), ((), ())),
                preferred_element_type=F32,
            )
            weights = jnp.exp2(scores).astype(BF16)
            accum[tile, lines, :] += jnp.dot(
                weights, vals[side, at, :], preferred_element_type=F32
            )
            return carry

        return lax.fori_loop(0, 2, part, carry)

    lax.fori_loop(0, 4 * tiles, advance, 0)
    for t in range(tiles):
        numerator, sums = collect(accum[t], tq, width)
        num_ref[t * tq : (t + 1) * tq, :] = numerator
        sum_ref[t * tq : (t + 1) * tq, :] = sums
    for n in (5, 14, 15, 16, 17):
        moves[n].wait_recv()
    for copy in exchanges + moves:
        copy.wait_send()
    for copy in [keep] + own_out:
        copy.wait()
    for p in range(4):
        for copy in hand_over(p):
            copy.wait()


def attend_kernel(
    tq, big, small,
    late_hbm, first_keys, first_a, first_b, query_hbm, raw_hbm, num_hbm, sum_hbm, wqkv_hbm,
    wout_hbm, whid_hbm, wback_hbm, note_ref, first_top, gain2_ref, out_ref,
    late, query, raw, num, sums_in, wkv, wout, whid, wback,
    keys, vals_a, vals_b, stacked, accum, top, key_top, sems,
):
    loops, half, width = late_hbm.shape
    slots = query_hbm.shape[0]
    head = width // HEADS
    kt = min(256, half)
    early_rows = loops * half
    scale = math.log2(math.e) / math.sqrt(head)
    me = lax.axis_index("loop")

    pairs = [(wqkv_hbm.at[:, pl.ds(width, 2 * width)], wkv)]
    pairs += [(late_hbm.at[j], late.at[j]) for j in range(loops)]
    pairs += [(query_hbm, query), (raw_hbm, raw), (num_hbm, num), (sum_hbm, sums_in)]
    pairs += [(wout_hbm, wout), (whid_hbm, whid), (wback_hbm, wback)]
    front = pl.ds(0, early_rows)
    pairs += [
        (first_keys, keys.at[front]), (first_a, vals_a.at[front]), (first_b, vals_b.at[front]),
    ]
    loads = [pltpu.make_async_copy(src, dst, sems.at[n]) for n, (src, dst) in enumerate(pairs)]
    for load in loads:
        load.start()
    out_ref[...] = jnp.zeros_like(out_ref)
    key_top[...] = first_top[...]

    def live_rows(j):
        note = note_ref[j].astype(F32)
        high, low = jnp.max(note[:, :128]), jnp.max(note[:, 128:])
        return (high * 128.0 + low).astype(jnp.int32)

    counts = [live_rows(j) for j in range(loops)]
    loads[0].wait()
    base = jnp.int32(early_rows)
    for j in range(loops):
        loads[1 + j].wait()
        count = jnp.maximum(counts[j] - half, 0)

        def tile(t, carry, j=j, base=base, count=count):
            start = pl.multiple_of(t * kt, kt)
            valid = iota((kt, width), 0) + start < count
            k, va, vb, peak = project(late[j, pl.ds(start, kt), :], wkv[...], valid, width)
            at = pl.ds(pl.multiple_of(base + start, 16), kt)
            keys[at, :] = k
            vals_a[at, :] = va
            vals_b[at, :] = vb
            key_top[...] = jnp.maximum(key_top[...], peak)
            return carry

        lax.fori_loop(0, pl.cdiv(count, kt), tile, 0)
        base = base + pl.cdiv(count, 16) * 16

    total_rows = base
    tail = pl.ds(pl.multiple_of(total_rows, 16), small)
    for ref in (keys, vals_a, vals_b):
        ref[tail, :] = jnp.zeros((small, width), BF16)
    highest = jnp.max(key_top[...], axis=0, keepdims=True)
    for load in loads[1 + loops : -3]:
        load.wait()

    mine = live_rows(me)
    to_head = one_hot(iota((width, 128), 0) // head == iota((width, 128), 1))
    flag_lane = one_hot(iota((8, width), 1) == head)
    reach = (jnp.abs(query[...].astype(F32)) * highest).astype(BF16)
    bound = jnp.max(jnp.dot(reach, to_head, preferred_element_type=F32))
    unshifted = bound * (1.02 * scale) < 90.0

    def wait_early(condition):
        @pl.when(condition)
        def _():
            for load in loads[-3:]:
                load.wait()

    wait_early(jnp.logical_not(unshifted))

    def queries(tq, start):
        group = HEADS // 2 * tq
        at_q = pl.ds(start, tq)
        q = query[at_q, :]
        lane_head = iota((tq, width), 1) // head
        for n, h in enumerate(head_order()):
            stacked[n * tq : (n + 1) * tq, :] = jnp.where(lane_head == h, q, jnp.zeros_like(q))
        accum[: 2 * group, :] = jnp.zeros((2 * group, width), F32)
        halves = ((slice(0, group), vals_a), (slice(group, 2 * group), vals_b))
        begun = jnp.logical_and(unshifted, start < half)
        first = jnp.where(begun, early_rows, 0)
        blocks = pl.cdiv(total_rows - first, small)

        def scores(at, rows):
            return scale * lax.dot_general(
                stacked[rows, :], keys[at, :], (((1,), (1,)), ((), ())), preferred_element_type=F32
            )

        def plain(size, offset):
            at = pl.ds(pl.multiple_of(offset, 16), size)
            for rows, vals in halves:
                weights = jnp.exp2(scores(at, rows)).astype(BF16)
                accum[rows, :] += jnp.dot(weights, vals[at, :], preferred_element_type=F32)

        def shifted(j, carry):
            at = pl.ds(pl.multiple_of(j * small, small), small)
            flags = lax.dot_general(
                flag_lane, vals_a[at, :], (((1,), (1,)), ((), ())), preferred_element_type=F32
            )
            live = flags[0:1, :] > 0.5
            for rows, vals in halves:
                values = jnp.where(live, scores(at, rows), -1e30)
                old = top[rows, :]
                new = jnp.maximum(old, jnp.max(values, axis=1, keepdims=True))
                top[rows, :] = new
                factor = jnp.exp2(old - new)
                weights = jnp.exp2(values - new[:, :1]).astype(BF16)
                accum[rows, :] = accum[rows, :] * factor[:, :1] + jnp.dot(
                    weights, vals[at, :], preferred_element_type=F32
                )
            return carry

        @pl.when(unshifted)
        def _():
            per = big // small
            many = blocks // per

            def step(j, carry):
                plain(big, first + j * big)
                return carry

            lax.fori_loop(0, many, step, 0)
            left = blocks - many * per
            offset = first + many * big
            size = big // 2
            while size >= small:
                units = size // small
                taken = left >= units

                @pl.when(taken)
                def _(size=size, offset=offset):
                    plain(size, offset)

                left = jnp.where(taken, left - units, left)
                offset = jnp.where(taken, offset + size, offset)
                size //= 2

        @pl.when(jnp.logical_not(unshifted))
        def _():
            top[: 2 * group, :] = jnp.full((2 * group, 128), -1e30, F32)
            lax.fori_loop(0, blocks, shifted, 0)

        numerator, sums = collect(accum[: 2 * group, :], tq, width)
        at_p = pl.ds(pl.multiple_of(jnp.where(start < half, start, 0), 16), tq)
        numerator = numerator + jnp.where(begun, num[at_p, :], 0.0)
        sums = sums + jnp.where(begun, sums_in[at_p, :], 0.0)
        even = even_lane((tq, width), head)
        total = jnp.where(
            even, pltpu.roll(sums, width - head, 1), pltpu.roll(sums, head, 1)
        )
        attended = (numerator / total).astype(BF16)
        mixed = raw[at_q, :].astype(F32) + jnp.dot(
            attended, wout[...], preferred_element_type=F32
        )
        normed2 = normalize(mixed, gain2_ref[...]).astype(BF16)
        inner = jnp.dot(normed2, whid[...], preferred_element_type=F32)
        hidden = (0.5 * inner * (1.0 + lax.erf(inner * math.sqrt(0.5)))).astype(BF16)
        result = mixed + jnp.dot(hidden, wback[...], preferred_element_type=F32)
        out_ref[at_q, :] = result.astype(BF16)

    tiles = pl.cdiv(mine, tq)
    begun_tiles = half // tq

    def each_tile(i, carry):
        wait_early(jnp.logical_and(unshifted, i == begun_tiles))
        queries(tq, pl.multiple_of(i * tq, tq))
        return carry

    lax.fori_loop(0, tiles, each_tile, 0)
    wait_early(jnp.logical_and(unshifted, tiles <= begun_tiles))


def give_back_kernel(
    regions, loops, result_ref, rank_ref, place_ref, out_ref, outbox, inbox, send, recv
):
    rows = out_ref.shape[0]
    chunk = CAP * loops
    slots = regions * chunk
    region, loop = lax.axis_index("region"), lax.axis_index("loop")
    barrier = pltpu.get_barrier_semaphore()
    for k in range(1, regions):
        pl.semaphore_signal(
            barrier, inc=1, device_id=(lax.rem(region + k, regions), loop), device_id_type=MESH
        )

    def column(row_ref):
        size = row_ref.shape[1]
        row = jnp.broadcast_to(row_ref[0:1, :].astype(F32), (128, size))
        return row.T[:, 0:1].astype(jnp.int32)

    unpack = one_hot(column(rank_ref) == iota((slots, slots), 1))
    outbox[...] = jnp.dot(unpack, result_ref[...], preferred_element_type=F32).astype(BF16)
    pl.semaphore_wait(barrier, regions - 1)

    def exchange(k):
        peer = lax.rem(region + k, regions)
        return pltpu.make_async_remote_copy(
            src_ref=outbox.at[pl.ds(pl.multiple_of(peer * chunk, chunk), chunk)],
            dst_ref=inbox.at[pl.ds(pl.multiple_of(region * chunk, chunk), chunk)],
            send_sem=send.at[k],
            recv_sem=recv.at[k],
            device_id=(peer, loop),
            device_id_type=MESH,
        )

    exchanges = [exchange(k) for k in range(1, regions)]
    for copy in exchanges:
        copy.start()
    own = pl.ds(pl.multiple_of(region * chunk, chunk), chunk)
    inbox[own, :] = outbox[own, :]
    take = one_hot(column(place_ref) == iota((rows, slots), 1))
    for copy in exchanges:
        copy.wait_recv()
    out_ref[...] = jnp.dot(take, inbox[...], preferred_element_type=F32).astype(BF16)
    for copy in exchanges:
        copy.wait_send()


def local(
    tiles, tokens, dest, norm1_gain, w_qkv, w_out, norm2_gain, w_hidden, w_back
):
    tq, big, small = tiles
    rows, width = tokens.shape
    regions, loops = lax.axis_size("region"), lax.axis_size("loop")
    chunk = CAP * loops
    slots = regions * chunk
    half = slots // 2
    vmem = pl.BlockSpec(memory_space=pltpu.VMEM)
    hbm = pl.BlockSpec(memory_space=pltpu.HBM)
    full = 62 * 1024 * 1024
    params = pltpu.CompilerParams
    shape = jax.ShapeDtypeStruct
    (
        late, first_keys, first_a, first_b, query, raw, notes, num, sums, key_top, place, rank,
    ) = pl.pallas_call(
        functools.partial(route_kernel, regions, loops, tq),
        out_shape=(
            shape((loops, half, width), BF16),
            shape((loops * half, width), BF16),
            shape((loops * half, width), BF16),
            shape((loops * half, width), BF16),
            shape((slots, width), BF16),
            shape((slots, width), BF16),
            shape((loops, EXTRA, width), BF16),
            shape((half, width), F32),
            shape((half, width), F32),
            shape((8, width), F32),
            shape((8, rows), jnp.int32),
            shape((8, slots), jnp.int32),
        ),
        in_specs=[vmem] * 4,
        out_specs=(hbm,) * 6 + (vmem,) * 6,
        scratch_shapes=[
            pltpu.VMEM((slots, width), BF16),
            pltpu.VMEM((slots, width), BF16),
            pltpu.VMEM((slots, width), BF16),
            pltpu.VMEM((slots, width), BF16),
            pltpu.VMEM((loops, half + EXTRA, width), BF16),
            pltpu.VMEM((half, width), BF16),
            pltpu.VMEM((loops * half, width), BF16),
            pltpu.VMEM((2, loops * half, width), BF16),
            pltpu.VMEM((half // tq, HEADS * tq, width), BF16),
            pltpu.VMEM((half // tq, HEADS * tq, width), F32),
            pltpu.SemaphoreType.DMA((regions,)),
            pltpu.SemaphoreType.DMA((regions,)),
            pltpu.SemaphoreType.DMA((18,)),
            pltpu.SemaphoreType.DMA((18,)),
            pltpu.SemaphoreType.DMA((15,)),
        ],
        compiler_params=params(vmem_limit_bytes=full, collective_id=0, has_side_effects=True),
        name="route",
    )(tokens, dest.reshape(1, rows), norm1_gain.reshape(1, width), w_qkv)
    key_rows = loops * slots + small + min(256, half)
    result = pl.pallas_call(
        functools.partial(attend_kernel, *tiles),
        out_shape=shape((slots, width), BF16),
        in_specs=[hbm] * 12 + [vmem] * 3,
        out_specs=vmem,
        scratch_shapes=[
            pltpu.VMEM((loops, half, width), BF16),
            pltpu.VMEM((slots, width), BF16),
            pltpu.VMEM((slots, width), BF16),
            pltpu.VMEM((half, width), F32),
            pltpu.VMEM((half, width), F32),
            pltpu.VMEM((width, 2 * width), BF16),
            pltpu.VMEM(w_out.shape, BF16),
            pltpu.VMEM(w_hidden.shape, BF16),
            pltpu.VMEM(w_back.shape, BF16),
            pltpu.VMEM((key_rows, width), BF16),
            pltpu.VMEM((key_rows, width), BF16),
            pltpu.VMEM((key_rows, width), BF16),
            pltpu.VMEM((HEADS * tq, width), BF16),
            pltpu.VMEM((HEADS * tq, width), F32),
            pltpu.VMEM((HEADS * tq, 128), F32),
            pltpu.VMEM((8, width), F32),
            pltpu.SemaphoreType.DMA((loops + 11,)),
        ],
        compiler_params=params(vmem_limit_bytes=full),
        name="attend",
    )(
        late, first_keys, first_a, first_b, query, raw, num, sums, w_qkv, w_out, w_hidden,
        w_back, notes, key_top, norm2_gain.reshape(1, width),
    )
    return pl.pallas_call(
        functools.partial(give_back_kernel, regions, loops),
        out_shape=jax.ShapeDtypeStruct((rows, width), BF16),
        in_specs=[vmem] * 3,
        out_specs=vmem,
        scratch_shapes=[
            pltpu.VMEM((slots, width), BF16),
            pltpu.VMEM((slots, width), BF16),
            pltpu.SemaphoreType.DMA((regions,)),
            pltpu.SemaphoreType.DMA((regions,)),
        ],
        compiler_params=params(vmem_limit_bytes=32 * 1024 * 1024, collective_id=1, has_side_effects=True),
        name="give_back",
    )(result, rank, place)


def build(mesh, tiles):
    spread = P(("region", "loop"), None)
    return jax.shard_map(
        functools.partial(local, tiles),
        mesh=mesh,
        in_specs=(spread, spread) + (P(),) * 6,
        out_specs=spread,
        check_vma=False,
    )


def solution(mesh):
    return build(mesh, (256, 2048, 512))
```

```python
import functools
import math

import jax
import jax.numpy as jnp
from jax import lax
from jax.experimental import pallas as pl
from jax.experimental.pallas import tpu as pltpu
from jax.sharding import PartitionSpec as P

HEADS = 8
CAP = 8
MARK = 16.0
MESH = pl.DeviceIdType.MESH
EXTRA = 16
F32 = jnp.float32
BF16 = jnp.bfloat16


def iota(shape, dim):
    return lax.broadcasted_iota(jnp.int32, shape, dim)


def one_hot(condition):
    return jnp.where(condition, 1.0, 0.0).astype(BF16)


def normalize(values, gain):
    mean = jnp.mean(values, axis=-1, keepdims=True)
    centered = values - mean
    variance = jnp.mean(centered * centered, axis=-1, keepdims=True)
    return centered * lax.rsqrt(variance + 1e-05) * gain


def head_order():
    return tuple(range(0, HEADS, 2)) + tuple(range(1, HEADS, 2))


def even_lane(shape, head):
    return lax.rem(iota(shape, 1) // head, 2) == 0


def project(rows, w_kv, valid, width):
    kv = jnp.dot(rows, w_kv, preferred_element_type=F32)
    k, v = kv[:, :width], kv[:, width:]
    even = even_lane(v.shape, width // HEADS)
    with_odd = jnp.where(valid, jnp.where(even, v, 1.0), 0.0).astype(BF16)
    with_even = jnp.where(valid, jnp.where(even, 1.0, v), 0.0).astype(BF16)
    peak = jnp.max(jnp.abs(k).reshape(k.shape[0] // 8, 8, width), axis=0)
    return k.astype(BF16), with_odd, with_even, peak


def collect(block, tq, width):
    group = HEADS // 2 * tq
    pair = iota((tq, width), 1) // (2 * (width // HEADS))
    part_a = jnp.zeros((tq, width), F32)
    part_b = jnp.zeros((tq, width), F32)
    for n in range(HEADS // 2):
        part_a = jnp.where(pair == n, block[n * tq : (n + 1) * tq, :], part_a)
        part_b = jnp.where(pair == n, block[group + n * tq : group + (n + 1) * tq, :], part_b)
    even = even_lane((tq, width), width // HEADS)
    return jnp.where(even, part_a, part_b), jnp.where(even, part_b, part_a)


def route_kernel(
    regions, loops, tq, tokens_ref, dest_ref, gain1_ref, wqkv_ref,
    late_ref, first_keys, first_a, first_b, query_ref, raw_ref, note_ref, num_ref, sum_ref,
    key_top, place_ref, rank_ref,
    outbox, inbox, query, raw, pool, own_late, keys, vals, stacked, accum,
    send_a, recv_a, send_g, recv_g, local_sem,
):
    rows, width = tokens_ref.shape
    chunk = CAP * loops
    slots = regions * chunk
    half = slots // 2
    chips = loops // 2
    head = width // HEADS
    scale = math.log2(math.e) / math.sqrt(head)
    region, loop = lax.axis_index("region"), lax.axis_index("loop")
    chip, core = loop // 2, lax.rem(loop, 2)
    sibling = chip * 2 + (1 - core)
    right_chip, left_chip = lax.rem(chip + 1, chips), lax.rem(chip + chips - 1, chips)
    far_chip = lax.rem(chip + 2, chips)
    right, left, far = right_chip * 2 + core, left_chip * 2 + core, far_chip * 2 + core

    barrier = pltpu.get_barrier_semaphore()
    for k in range(1, regions):
        pl.semaphore_signal(
            barrier, inc=1, device_id=(lax.rem(region + k, regions), loop), device_id_type=MESH
        )
    for peer in (sibling, left, right):
        pl.semaphore_signal(barrier, inc=1, device_id=(region, peer), device_id_type=MESH)

    owner_region = dest_ref[...] // loops
    hot = one_hot(owner_region == iota((regions, rows), 0))
    not_later = one_hot(iota((rows, rows), 0) <= iota((rows, rows), 1))
    before = jnp.dot(hot, not_later, preferred_element_type=F32)
    rank = jnp.sum(before * hot.astype(F32), axis=0, keepdims=True).astype(jnp.int32) - 1
    place = owner_region * chunk + rank
    place_ref[...] = jnp.broadcast_to(place, place_ref.shape)
    spread = one_hot(iota((slots, rows), 0) == place)
    sorted_rows = jnp.dot(spread, tokens_ref[...], preferred_element_type=F32)
    held = jnp.dot(spread, jnp.ones((rows, width), BF16), preferred_element_type=F32)
    outbox[...] = (sorted_rows + (1.0 - held) * MARK).astype(BF16)

    pl.semaphore_wait(barrier, regions - 1 + 3)

    def exchange(k):
        peer = lax.rem(region + k, regions)
        return pltpu.make_async_remote_copy(
            src_ref=outbox.at[pl.ds(pl.multiple_of(peer * chunk, chunk), chunk)],
            dst_ref=inbox.at[pl.ds(pl.multiple_of(region * chunk, chunk), chunk)],
            send_sem=send_a.at[k],
            recv_sem=recv_a.at[k],
            device_id=(peer, loop),
            device_id_type=MESH,
        )

    exchanges = [exchange(k) for k in range(1, regions)]
    for copy in exchanges:
        copy.start()
    own = pl.ds(pl.multiple_of(region * chunk, chunk), chunk)
    inbox[own, :] = outbox[own, :]
    earlier = one_hot(iota((slots, slots), 0) < iota((slots, slots), 1))

    for copy in exchanges:
        copy.wait_recv()
    landed = inbox[...]
    normed = normalize(landed.astype(F32), gain1_ref[...]).astype(BF16)

    alive = jnp.where(landed[:, :128].astype(F32) < 8.0, 1.0, 0.0)
    alive_row = alive.T[:16, :]
    ahead = jnp.dot(alive_row.astype(BF16), earlier, preferred_element_type=F32)
    slot = jnp.where(alive_row > 0.0, ahead, -1.0).astype(jnp.int32)
    rank_ref[...] = slot[:8, :]
    squeeze = one_hot(iota((slots, slots), 0) == slot[0:1, :])
    packed = jnp.dot(squeeze, normed, preferred_element_type=F32).astype(BF16)
    count = jnp.sum(alive_row, axis=1, keepdims=True)
    tens = jnp.floor(count * (1.0 / 128.0))
    pool[loop, pl.ds(0, EXTRA), :] = jnp.where(
        iota((EXTRA, width), 1) < 128, tens, count - 128.0 * tens
    ).astype(BF16)
    pool[loop, pl.ds(EXTRA, half), :] = packed[:half, :]
    own_late[...] = packed[half:, :]

    def move(n, src, dst, peer):
        return pltpu.make_async_remote_copy(
            src_ref=src,
            dst_ref=dst,
            send_sem=send_g.at[n],
            recv_sem=recv_g.at[n],
            device_id=(region, peer),
            device_id_type=MESH,
        )

    quarter = half // 2
    upper, lower = pl.ds(0, EXTRA + quarter), pl.ds(EXTRA + quarter, quarter)
    high, low = pl.ds(0, quarter), pl.ds(quarter, quarter)

    def early(n, index, peer, *part):
        return move(n, pool.at[(index, *part)], pool.at[(index, *part)], peer)

    def late(n, index, peer, *part):
        return move(n, late_ref.at[(index, *part)], late_ref.at[(index, *part)], peer)

    moves = [
        early(0, loop, right),
        early(1, loop, left),
        early(2, loop, sibling),
        move(3, own_late, late_ref.at[loop], right),
        move(4, own_late, late_ref.at[loop], left),
        move(5, own_late, late_ref.at[loop], sibling),
        early(6, left, right, upper),
        early(7, right, left, lower),
        early(8, left, sibling),
        early(9, right, sibling),
        early(10, far, sibling, upper),
        early(11, far, sibling, lower),
        late(12, left, right, high),
        late(13, right, left, low),
        late(14, left, sibling),
        late(15, right, sibling),
        late(16, far, sibling, high),
        late(17, far, sibling, low),
    ]
    for n in range(3):
        moves[n].start()
    keep = pltpu.make_async_copy(own_late, late_ref.at[loop], local_sem.at[0])
    keep.start()

    own_rows = jnp.concatenate([pool[loop, pl.ds(EXTRA, half), :], own_late[...]], axis=0)
    q_all = jnp.dot(own_rows, wqkv_ref[:, :width], preferred_element_type=F32).astype(BF16)
    query[...] = q_all
    tiles = half // tq
    lane_head = iota((tq, width), 1) // head
    for t in range(tiles):
        q = q_all[t * tq : (t + 1) * tq, :]
        for n, h in enumerate(head_order()):
            stacked[t, n * tq : (n + 1) * tq, :] = jnp.where(lane_head == h, q, jnp.zeros_like(q))
    raw[...] = jnp.dot(squeeze, landed, preferred_element_type=F32).astype(BF16)
    own_out = [
        pltpu.make_async_copy(query, query_ref, local_sem.at[13]),
        pltpu.make_async_copy(raw, raw_ref, local_sem.at[14]),
    ]
    for copy in own_out:
        copy.start()
    accum[...] = jnp.zeros_like(accum)
    key_top[...] = jnp.zeros_like(key_top)

    group = HEADS // 2 * tq

    def hand_over(p):
        at = pl.ds(pl.multiple_of(2 * p * half, 2 * half), 2 * half)
        return [
            pltpu.make_async_copy(src.at[at], dst.at[at], local_sem.at[1 + 3 * p + n])
            for n, (src, dst) in enumerate(
                ((keys, first_keys), (vals.at[0], first_a), (vals.at[1], first_b))
            )
        ]

    def prepare(p):
        turn = jnp.where(p == 1, chips - 1, jnp.where(p == 2, 1, jnp.where(p == 3, 2, 0)))

        def one(c, carry):
            j = lax.rem(chip + turn, chips) * 2 + lax.rem(core + c, 2)
            note = pool[j, pl.ds(0, EXTRA), :]
            note_ref[j] = note
            note = note.astype(F32)
            live = note[0:1, 0:1] * 128.0 + note[0:1, 128:129]
            valid = iota((half, width), 0).astype(F32) < live
            k, va, vb, peak = project(
                pool[j, pl.ds(EXTRA, half), :], wqkv_ref[:, width:], valid, width
            )
            at = pl.ds(pl.multiple_of((2 * p + c) * half, half), half)
            keys[at, :] = k
            vals[0, at, :] = va
            vals[1, at, :] = vb
            key_top[...] = jnp.maximum(key_top[...], peak)
            return carry

        lax.fori_loop(0, 2, one, 0)
        for copy in hand_over(p):
            copy.start()

    script = {
        0: ((2,), ()),
        1: ((0, 1), (6, 7, 8, 9, 3, 4, 5)),
        tiles: ((8,), ()),
        tiles + 1: ((6, 7), (10, 11)),
        2 * tiles: ((9,), ()),
        2 * tiles + 1: ((3, 4), (12, 13, 14, 15)),
        3 * tiles: ((10, 11), ()),
        3 * tiles + 1: ((12, 13), (16, 17)),
    }

    def advance(step, carry):
        p, tile = step // tiles, lax.rem(step, tiles)
        for when, (arrived, onward) in script.items():

            @pl.when(step == when)
            def _(arrived=arrived, onward=onward):
                for n in arrived:
                    moves[n].wait_recv()
                for n in onward:
                    moves[n].start()

        @pl.when(tile == 0)
        def _():
            prepare(p)

        at = pl.ds(pl.multiple_of(2 * p * half, 2 * half), 2 * half)

        def weights(side):
            scores = scale * lax.dot_general(
                stacked[tile, side * group : (side + 1) * group, :], keys[at, :],
                (((1,), (1,)), ((), ())), preferred_element_type=F32,
            )
            return jnp.exp2(scores).astype(BF16)

        def add(side, parts):
            accum[tile, side * group : (side + 1) * group, :] += jnp.dot(
                parts, vals[side, at, :], preferred_element_type=F32
            )

        parts_a = weights(0)
        parts_b = weights(1)
        add(0, parts_a)
        add(1, parts_b)
        return carry

    lax.fori_loop(0, 4 * tiles, advance, 0)
    for t in range(tiles):
        numerator, sums = collect(accum[t], tq, width)
        num_ref[t * tq : (t + 1) * tq, :] = numerator
        sum_ref[t * tq : (t + 1) * tq, :] = sums
    for n in (5, 14, 15, 16, 17):
        moves[n].wait_recv()
    for copy in exchanges + moves:
        copy.wait_send()
    for copy in [keep] + own_out:
        copy.wait()
    for p in range(4):
        for copy in hand_over(p):
            copy.wait()


def attend_kernel(
    tq, big, small,
    late_hbm, first_keys, first_a, first_b, query_hbm, raw_hbm, num_hbm, sum_hbm, wqkv_hbm,
    wout_hbm, whid_hbm, wback_hbm, note_ref, first_top, gain2_ref, out_ref,
    late, query, raw, num, sums_in, wkv, wout, whid, wback,
    keys, vals_a, vals_b, stacked, accum, top, key_top, sems,
):
    loops, half, width = late_hbm.shape
    slots = query_hbm.shape[0]
    head = width // HEADS
    kt = min(256, half)
    early_rows = loops * half
    scale = math.log2(math.e) / math.sqrt(head)
    me = lax.axis_index("loop")

    pairs = [(wqkv_hbm.at[:, pl.ds(width, 2 * width)], wkv)]
    pairs += [(late_hbm.at[j], late.at[j]) for j in range(loops)]
    pairs += [(query_hbm, query), (raw_hbm, raw), (num_hbm, num), (sum_hbm, sums_in)]
    pairs += [(wout_hbm, wout), (whid_hbm, whid), (wback_hbm, wback)]
    front = pl.ds(0, early_rows)
    pairs += [
        (first_keys, keys.at[front]), (first_a, vals_a.at[front]), (first_b, vals_b.at[front]),
    ]
    loads = [pltpu.make_async_copy(src, dst, sems.at[n]) for n, (src, dst) in enumerate(pairs)]
    for load in loads:
        load.start()
    out_ref[...] = jnp.zeros_like(out_ref)
    key_top[...] = first_top[...]

    def live_rows(j):
        note = note_ref[j].astype(F32)
        high, low = jnp.max(note[:, :128]), jnp.max(note[:, 128:])
        return (high * 128.0 + low).astype(jnp.int32)

    counts = [live_rows(j) for j in range(loops)]
    loads[0].wait()
    base = jnp.int32(early_rows)
    for j in range(loops):
        loads[1 + j].wait()
        count = jnp.maximum(counts[j] - half, 0)

        def tile(t, carry, j=j, base=base, count=count):
            start = pl.multiple_of(t * kt, kt)
            valid = iota((kt, width), 0) + start < count
            k, va, vb, peak = project(late[j, pl.ds(start, kt), :], wkv[...], valid, width)
            at = pl.ds(pl.multiple_of(base + start, 16), kt)
            keys[at, :] = k
            vals_a[at, :] = va
            vals_b[at, :] = vb
            key_top[...] = jnp.maximum(key_top[...], peak)
            return carry

        lax.fori_loop(0, pl.cdiv(count, kt), tile, 0)
        base = base + pl.cdiv(count, 16) * 16

    total_rows = base
    tail = pl.ds(pl.multiple_of(total_rows, 16), small)
    for ref in (keys, vals_a, vals_b):
        ref[tail, :] = jnp.zeros((small, width), BF16)
    highest = jnp.max(key_top[...], axis=0, keepdims=True)
    for load in loads[1 + loops : -3]:
        load.wait()

    mine = live_rows(me)
    to_head = one_hot(iota((width, 128), 0) // head == iota((width, 128), 1))
    flag_lane = one_hot(iota((8, width), 1) == head)
    reach = (jnp.abs(query[...].astype(F32)) * highest).astype(BF16)
    bound = jnp.max(jnp.dot(reach, to_head, preferred_element_type=F32))
    unshifted = bound * (1.02 * scale) < 90.0

    def wait_early(condition):
        @pl.when(condition)
        def _():
            for load in loads[-3:]:
                load.wait()

    wait_early(jnp.logical_not(unshifted))

    def queries(tq, start):
        group = HEADS // 2 * tq
        at_q = pl.ds(start, tq)
        q = query[at_q, :]
        lane_head = iota((tq, width), 1) // head
        for n, h in enumerate(head_order()):
            stacked[n * tq : (n + 1) * tq, :] = jnp.where(lane_head == h, q, jnp.zeros_like(q))
        accum[: 2 * group, :] = jnp.zeros((2 * group, width), F32)
        halves = ((slice(0, group), vals_a), (slice(group, 2 * group), vals_b))
        begun = jnp.logical_and(unshifted, start < half)
        first = jnp.where(begun, early_rows, 0)
        blocks = pl.cdiv(total_rows - first, small)

        def scores(at, rows):
            return scale * lax.dot_general(
                stacked[rows, :], keys[at, :], (((1,), (1,)), ((), ())), preferred_element_type=F32
            )

        def plain(size, offset):
            at = pl.ds(pl.multiple_of(offset, 16), size)
            parts = [jnp.exp2(scores(at, rows)).astype(BF16) for rows, vals in halves]
            for (rows, vals), part in zip(halves, parts):
                accum[rows, :] += jnp.dot(part, vals[at, :], preferred_element_type=F32)

        def shifted(j, carry):
            at = pl.ds(pl.multiple_of(j * small, small), small)
            flags = lax.dot_general(
                flag_lane, vals_a[at, :], (((1,), (1,)), ((), ())), preferred_element_type=F32
            )
            live = flags[0:1, :] > 0.5
            for rows, vals in halves:
                values = jnp.where(live, scores(at, rows), -1e30)
                old = top[rows, :]
                new = jnp.maximum(old, jnp.max(values, axis=1, keepdims=True))
                top[rows, :] = new
                factor = jnp.exp2(old - new)
                weights = jnp.exp2(values - new[:, :1]).astype(BF16)
                accum[rows, :] = accum[rows, :] * factor[:, :1] + jnp.dot(
                    weights, vals[at, :], preferred_element_type=F32
                )
            return carry

        @pl.when(unshifted)
        def _():
            per = big // small
            many = blocks // per

            def step(j, carry):
                plain(big, first + j * big)
                return carry

            lax.fori_loop(0, many, step, 0)
            left = blocks - many * per
            offset = first + many * big
            size = big // 2
            while size >= small:
                units = size // small
                taken = left >= units

                @pl.when(taken)
                def _(size=size, offset=offset):
                    plain(size, offset)

                left = jnp.where(taken, left - units, left)
                offset = jnp.where(taken, offset + size, offset)
                size //= 2

        @pl.when(jnp.logical_not(unshifted))
        def _():
            top[: 2 * group, :] = jnp.full((2 * group, 128), -1e30, F32)
            lax.fori_loop(0, blocks, shifted, 0)

        numerator, sums = collect(accum[: 2 * group, :], tq, width)
        at_p = pl.ds(pl.multiple_of(jnp.where(start < half, start, 0), 16), tq)
        numerator = numerator + jnp.where(begun, num[at_p, :], 0.0)
        sums = sums + jnp.where(begun, sums_in[at_p, :], 0.0)
        even = even_lane((tq, width), head)
        total = jnp.where(
            even, pltpu.roll(sums, width - head, 1), pltpu.roll(sums, head, 1)
        )
        attended = (numerator / total).astype(BF16)
        mixed = raw[at_q, :].astype(F32) + jnp.dot(
            attended, wout[...], preferred_element_type=F32
        )
        normed2 = normalize(mixed, gain2_ref[...]).astype(BF16)
        inner = jnp.dot(normed2, whid[...], preferred_element_type=F32)
        hidden = (0.5 * inner * (1.0 + lax.erf(inner * math.sqrt(0.5)))).astype(BF16)
        result = mixed + jnp.dot(hidden, wback[...], preferred_element_type=F32)
        out_ref[at_q, :] = result.astype(BF16)

    tiles = pl.cdiv(mine, tq)
    begun_tiles = half // tq

    def each_tile(i, carry):
        wait_early(jnp.logical_and(unshifted, i == begun_tiles))
        queries(tq, pl.multiple_of(i * tq, tq))
        return carry

    lax.fori_loop(0, tiles, each_tile, 0)
    wait_early(jnp.logical_and(unshifted, tiles <= begun_tiles))


def give_back_kernel(
    regions, loops, result_ref, rank_ref, place_ref, out_ref, outbox, inbox, send, recv
):
    rows = out_ref.shape[0]
    chunk = CAP * loops
    slots = regions * chunk
    region, loop = lax.axis_index("region"), lax.axis_index("loop")
    barrier = pltpu.get_barrier_semaphore()
    for k in range(1, regions):
        pl.semaphore_signal(
            barrier, inc=1, device_id=(lax.rem(region + k, regions), loop), device_id_type=MESH
        )

    def column(row_ref):
        size = row_ref.shape[1]
        row = jnp.broadcast_to(row_ref[0:1, :].astype(F32), (128, size))
        return row.T[:, 0:1].astype(jnp.int32)

    unpack = one_hot(column(rank_ref) == iota((slots, slots), 1))
    outbox[...] = jnp.dot(unpack, result_ref[...], preferred_element_type=F32).astype(BF16)
    pl.semaphore_wait(barrier, regions - 1)

    def exchange(k):
        peer = lax.rem(region + k, regions)
        return pltpu.make_async_remote_copy(
            src_ref=outbox.at[pl.ds(pl.multiple_of(peer * chunk, chunk), chunk)],
            dst_ref=inbox.at[pl.ds(pl.multiple_of(region * chunk, chunk), chunk)],
            send_sem=send.at[k],
            recv_sem=recv.at[k],
            device_id=(peer, loop),
            device_id_type=MESH,
        )

    exchanges = [exchange(k) for k in range(1, regions)]
    for copy in exchanges:
        copy.start()
    own = pl.ds(pl.multiple_of(region * chunk, chunk), chunk)
    inbox[own, :] = outbox[own, :]
    take = one_hot(column(place_ref) == iota((rows, slots), 1))
    for copy in exchanges:
        copy.wait_recv()
    out_ref[...] = jnp.dot(take, inbox[...], preferred_element_type=F32).astype(BF16)
    for copy in exchanges:
        copy.wait_send()


def local(
    tiles, tokens, dest, norm1_gain, w_qkv, w_out, norm2_gain, w_hidden, w_back
):
    tq, big, small = tiles
    rows, width = tokens.shape
    regions, loops = lax.axis_size("region"), lax.axis_size("loop")
    chunk = CAP * loops
    slots = regions * chunk
    half = slots // 2
    vmem = pl.BlockSpec(memory_space=pltpu.VMEM)
    hbm = pl.BlockSpec(memory_space=pltpu.HBM)
    full = 62 * 1024 * 1024
    params = pltpu.CompilerParams
    shape = jax.ShapeDtypeStruct
    (
        late, first_keys, first_a, first_b, query, raw, notes, num, sums, key_top, place, rank,
    ) = pl.pallas_call(
        functools.partial(route_kernel, regions, loops, tq),
        out_shape=(
            shape((loops, half, width), BF16),
            shape((loops * half, width), BF16),
            shape((loops * half, width), BF16),
            shape((loops * half, width), BF16),
            shape((slots, width), BF16),
            shape((slots, width), BF16),
            shape((loops, EXTRA, width), BF16),
            shape((half, width), F32),
            shape((half, width), F32),
            shape((8, width), F32),
            shape((8, rows), jnp.int32),
            shape((8, slots), jnp.int32),
        ),
        in_specs=[vmem] * 4,
        out_specs=(hbm,) * 6 + (vmem,) * 6,
        scratch_shapes=[
            pltpu.VMEM((slots, width), BF16),
            pltpu.VMEM((slots, width), BF16),
            pltpu.VMEM((slots, width), BF16),
            pltpu.VMEM((slots, width), BF16),
            pltpu.VMEM((loops, half + EXTRA, width), BF16),
            pltpu.VMEM((half, width), BF16),
            pltpu.VMEM((loops * half, width), BF16),
            pltpu.VMEM((2, loops * half, width), BF16),
            pltpu.VMEM((half // tq, HEADS * tq, width), BF16),
            pltpu.VMEM((half // tq, HEADS * tq, width), F32),
            pltpu.SemaphoreType.DMA((regions,)),
            pltpu.SemaphoreType.DMA((regions,)),
            pltpu.SemaphoreType.DMA((18,)),
            pltpu.SemaphoreType.DMA((18,)),
            pltpu.SemaphoreType.DMA((15,)),
        ],
        compiler_params=params(vmem_limit_bytes=full, collective_id=0, has_side_effects=True),
        name="route",
    )(tokens, dest.reshape(1, rows), norm1_gain.reshape(1, width), w_qkv)
    key_rows = loops * slots + small + min(256, half)
    result = pl.pallas_call(
        functools.partial(attend_kernel, *tiles),
        out_shape=shape((slots, width), BF16),
        in_specs=[hbm] * 12 + [vmem] * 3,
        out_specs=vmem,
        scratch_shapes=[
            pltpu.VMEM((loops, half, width), BF16),
            pltpu.VMEM((slots, width), BF16),
            pltpu.VMEM((slots, width), BF16),
            pltpu.VMEM((half, width), F32),
            pltpu.VMEM((half, width), F32),
            pltpu.VMEM((width, 2 * width), BF16),
            pltpu.VMEM(w_out.shape, BF16),
            pltpu.VMEM(w_hidden.shape, BF16),
            pltpu.VMEM(w_back.shape, BF16),
            pltpu.VMEM((key_rows, width), BF16),
            pltpu.VMEM((key_rows, width), BF16),
            pltpu.VMEM((key_rows, width), BF16),
            pltpu.VMEM((HEADS * tq, width), BF16),
            pltpu.VMEM((HEADS * tq, width), F32),
            pltpu.VMEM((HEADS * tq, 128), F32),
            pltpu.VMEM((8, width), F32),
            pltpu.SemaphoreType.DMA((loops + 11,)),
        ],
        compiler_params=params(vmem_limit_bytes=full),
        name="attend",
    )(
        late, first_keys, first_a, first_b, query, raw, num, sums, w_qkv, w_out, w_hidden,
        w_back, notes, key_top, norm2_gain.reshape(1, width),
    )
    return pl.pallas_call(
        functools.partial(give_back_kernel, regions, loops),
        out_shape=jax.ShapeDtypeStruct((rows, width), BF16),
        in_specs=[vmem] * 3,
        out_specs=vmem,
        scratch_shapes=[
            pltpu.VMEM((slots, width), BF16),
            pltpu.VMEM((slots, width), BF16),
            pltpu.SemaphoreType.DMA((regions,)),
            pltpu.SemaphoreType.DMA((regions,)),
        ],
        compiler_params=params(vmem_limit_bytes=32 * 1024 * 1024, collective_id=1, has_side_effects=True),
        name="give_back",
    )(result, rank, place)


def build(mesh, tiles):
    spread = P(("region", "loop"), None)
    return jax.shard_map(
        functools.partial(local, tiles),
        mesh=mesh,
        in_specs=(spread, spread) + (P(),) * 6,
        out_specs=spread,
        check_vma=False,
    )


def solution(mesh):
    return build(mesh, (256, 2048, 512))
```

```python
import functools
import math

import jax
import jax.numpy as jnp
from jax import lax
from jax.experimental import pallas as pl
from jax.experimental.pallas import tpu as pltpu
from jax.sharding import PartitionSpec as P

HEADS = 8
CAP = 8
MARK = 16.0
MESH = pl.DeviceIdType.MESH
EXTRA = 16
F32 = jnp.float32
BF16 = jnp.bfloat16


def iota(shape, dim):
    return lax.broadcasted_iota(jnp.int32, shape, dim)


def one_hot(condition):
    return jnp.where(condition, 1.0, 0.0).astype(BF16)


def normalize(values, gain):
    mean = jnp.mean(values, axis=-1, keepdims=True)
    centered = values - mean
    variance = jnp.mean(centered * centered, axis=-1, keepdims=True)
    return centered * lax.rsqrt(variance + 1e-05) * gain


def head_order():
    return tuple(range(0, HEADS, 2)) + tuple(range(1, HEADS, 2))


def even_lane(shape, head):
    return lax.rem(iota(shape, 1) // head, 2) == 0


def project(rows, w_kv, valid, width):
    kv = jnp.dot(rows, w_kv, preferred_element_type=F32)
    k, v = kv[:, :width], kv[:, width:]
    even = even_lane(v.shape, width // HEADS)
    with_odd = jnp.where(valid, jnp.where(even, v, 1.0), 0.0).astype(BF16)
    with_even = jnp.where(valid, jnp.where(even, 1.0, v), 0.0).astype(BF16)
    peak = jnp.max(jnp.abs(k).reshape(k.shape[0] // 8, 8, width), axis=0)
    return k.astype(BF16), with_odd, with_even, peak


def collect(block, tq, width):
    group = HEADS // 2 * tq
    pair = iota((tq, width), 1) // (2 * (width // HEADS))
    part_a = jnp.zeros((tq, width), F32)
    part_b = jnp.zeros((tq, width), F32)
    for n in range(HEADS // 2):
        part_a = jnp.where(pair == n, block[n * tq : (n + 1) * tq, :], part_a)
        part_b = jnp.where(pair == n, block[group + n * tq : group + (n + 1) * tq, :], part_b)
    even = even_lane((tq, width), width // HEADS)
    return jnp.where(even, part_a, part_b), jnp.where(even, part_b, part_a)


def route_kernel(
    regions, loops, tq, tokens_ref, dest_ref, gain1_ref, wqkv_ref,
    late_ref, first_keys, first_a, first_b, query_ref, raw_ref, note_ref, num_ref, sum_ref,
    key_top, place_ref, rank_ref,
    outbox, inbox, query, raw, pool, own_late, keys, vals, stacked, accum,
    send_a, recv_a, send_g, recv_g, local_sem,
):
    rows, width = tokens_ref.shape
    chunk = CAP * loops
    slots = regions * chunk
    half = slots // 2
    chips = loops // 2
    head = width // HEADS
    scale = math.log2(math.e) / math.sqrt(head)
    region, loop = lax.axis_index("region"), lax.axis_index("loop")
    chip, core = loop // 2, lax.rem(loop, 2)
    sibling = chip * 2 + (1 - core)
    right_chip, left_chip = lax.rem(chip + 1, chips), lax.rem(chip + chips - 1, chips)
    far_chip = lax.rem(chip + 2, chips)
    right, left, far = right_chip * 2 + core, left_chip * 2 + core, far_chip * 2 + core

    barrier = pltpu.get_barrier_semaphore()
    for k in range(1, regions):
        pl.semaphore_signal(
            barrier, inc=1, device_id=(lax.rem(region + k, regions), loop), device_id_type=MESH
        )
    for peer in (sibling, left, right):
        pl.semaphore_signal(barrier, inc=1, device_id=(region, peer), device_id_type=MESH)

    owner_region = dest_ref[...] // loops
    hot = one_hot(owner_region == iota((regions, rows), 0))
    not_later = one_hot(iota((rows, rows), 0) <= iota((rows, rows), 1))
    before = jnp.dot(hot, not_later, preferred_element_type=F32)
    rank = jnp.sum(before * hot.astype(F32), axis=0, keepdims=True).astype(jnp.int32) - 1
    place = owner_region * chunk + rank
    place_ref[...] = jnp.broadcast_to(place, place_ref.shape)
    spread = one_hot(iota((slots, rows), 0) == place)
    sorted_rows = jnp.dot(spread, tokens_ref[...], preferred_element_type=F32)
    held = jnp.dot(spread, jnp.ones((rows, width), BF16), preferred_element_type=F32)
    outbox[...] = (sorted_rows + (1.0 - held) * MARK).astype(BF16)

    pl.semaphore_wait(barrier, regions - 1 + 3)

    def exchange(k):
        peer = lax.rem(region + k, regions)
        return pltpu.make_async_remote_copy(
            src_ref=outbox.at[pl.ds(pl.multiple_of(peer * chunk, chunk), chunk)],
            dst_ref=inbox.at[pl.ds(pl.multiple_of(region * chunk, chunk), chunk)],
            send_sem=send_a.at[k],
            recv_sem=recv_a.at[k],
            device_id=(peer, loop),
            device_id_type=MESH,
        )

    exchanges = [exchange(k) for k in range(1, regions)]
    for copy in exchanges:
        copy.start()
    own = pl.ds(pl.multiple_of(region * chunk, chunk), chunk)
    inbox[own, :] = outbox[own, :]
    earlier = one_hot(iota((slots, slots), 0) < iota((slots, slots), 1))

    for copy in exchanges:
        copy.wait_recv()
    landed = inbox[...]
    normed = normalize(landed.astype(F32), gain1_ref[...]).astype(BF16)

    alive = jnp.where(landed[:, :128].astype(F32) < 8.0, 1.0, 0.0)
    alive_row = alive.T[:16, :]
    ahead = jnp.dot(alive_row.astype(BF16), earlier, preferred_element_type=F32)
    slot = jnp.where(alive_row > 0.0, ahead, -1.0).astype(jnp.int32)
    rank_ref[...] = slot[:8, :]
    squeeze = one_hot(iota((slots, slots), 0) == slot[0:1, :])
    packed = jnp.dot(squeeze, normed, preferred_element_type=F32).astype(BF16)
    count = jnp.sum(alive_row, axis=1, keepdims=True)
    tens = jnp.floor(count * (1.0 / 128.0))
    pool[loop, pl.ds(0, EXTRA), :] = jnp.where(
        iota((EXTRA, width), 1) < 128, tens, count - 128.0 * tens
    ).astype(BF16)
    pool[loop, pl.ds(EXTRA, half), :] = packed[:half, :]
    own_late[...] = packed[half:, :]

    def move(n, src, dst, peer):
        return pltpu.make_async_remote_copy(
            src_ref=src,
            dst_ref=dst,
            send_sem=send_g.at[n],
            recv_sem=recv_g.at[n],
            device_id=(region, peer),
            device_id_type=MESH,
        )

    quarter = half // 2
    upper, lower = pl.ds(0, EXTRA + quarter), pl.ds(EXTRA + quarter, quarter)
    high, low = pl.ds(0, quarter), pl.ds(quarter, quarter)

    def early(n, index, peer, *part):
        return move(n, pool.at[(index, *part)], pool.at[(index, *part)], peer)

    def late(n, index, peer, *part):
        return move(n, late_ref.at[(index, *part)], late_ref.at[(index, *part)], peer)

    moves = [
        early(0, loop, right),
        early(1, loop, left),
        early(2, loop, sibling),
        move(3, own_late, late_ref.at[loop], right),
        move(4, own_late, late_ref.at[loop], left),
        move(5, own_late, late_ref.at[loop], sibling),
        early(6, left, right, upper),
        early(7, right, left, lower),
        early(8, left, sibling),
        early(9, right, sibling),
        early(10, far, sibling, upper),
        early(11, far, sibling, lower),
        late(12, left, right, high),
        late(13, right, left, low),
        late(14, left, sibling),
        late(15, right, sibling),
        late(16, far, sibling, high),
        late(17, far, sibling, low),
    ]
    for n in range(3):
        moves[n].start()
    keep = pltpu.make_async_copy(own_late, late_ref.at[loop], local_sem.at[0])
    keep.start()

    own_rows = jnp.concatenate([pool[loop, pl.ds(EXTRA, half), :], own_late[...]], axis=0)
    q_all = jnp.dot(own_rows, wqkv_ref[:, :width], preferred_element_type=F32).astype(BF16)
    query[...] = q_all
    tiles = half // tq
    lane_head = iota((tq, width), 1) // head
    for t in range(tiles):
        q = q_all[t * tq : (t + 1) * tq, :]
        for n, h in enumerate(head_order()):
            stacked[t, n * tq : (n + 1) * tq, :] = jnp.where(lane_head == h, q, jnp.zeros_like(q))
    raw[...] = jnp.dot(squeeze, landed, preferred_element_type=F32).astype(BF16)
    own_out = [
        pltpu.make_async_copy(query, query_ref, local_sem.at[13]),
        pltpu.make_async_copy(raw, raw_ref, local_sem.at[14]),
    ]
    for copy in own_out:
        copy.start()
    accum[...] = jnp.zeros_like(accum)
    key_top[...] = jnp.zeros_like(key_top)

    group = HEADS // 2 * tq

    def hand_over(p):
        at = pl.ds(pl.multiple_of(2 * p * half, 2 * half), 2 * half)
        return [
            pltpu.make_async_copy(src.at[at], dst.at[at], local_sem.at[1 + 3 * p + n])
            for n, (src, dst) in enumerate(
                ((keys, first_keys), (vals.at[0], first_a), (vals.at[1], first_b))
            )
        ]

    def prepare(p):
        turn = jnp.where(p == 1, chips - 1, jnp.where(p == 2, 1, jnp.where(p == 3, 2, 0)))

        def one(c, carry):
            j = lax.rem(chip + turn, chips) * 2 + lax.rem(core + c, 2)
            note = pool[j, pl.ds(0, EXTRA), :]
            note_ref[j] = note
            note = note.astype(F32)
            live = note[0:1, 0:1] * 128.0 + note[0:1, 128:129]
            valid = iota((half, width), 0).astype(F32) < live
            k, va, vb, peak = project(
                pool[j, pl.ds(EXTRA, half), :], wqkv_ref[:, width:], valid, width
            )
            at = pl.ds(pl.multiple_of((2 * p + c) * half, half), half)
            keys[at, :] = k
            vals[0, at, :] = va
            vals[1, at, :] = vb
            key_top[...] = jnp.maximum(key_top[...], peak)
            return carry

        lax.fori_loop(0, 2, one, 0)
        for copy in hand_over(p):
            copy.start()

    script = {
        0: ((2,), ()),
        1: ((0, 1), (6, 7, 8, 9, 3, 4, 5)),
        tiles: ((8,), ()),
        tiles + 1: ((6, 7), (10, 11)),
        2 * tiles: ((9,), ()),
        2 * tiles + 1: ((3, 4), (12, 13, 14, 15)),
        3 * tiles: ((10, 11), ()),
        3 * tiles + 1: ((12, 13), (16, 17)),
    }

    def advance(step, carry):
        p, tile = step // tiles, lax.rem(step, tiles)
        for when, (arrived, onward) in script.items():

            @pl.when(step == when)
            def _(arrived=arrived, onward=onward):
                for n in arrived:
                    moves[n].wait_recv()
                for n in onward:
                    moves[n].start()

        @pl.when(tile == 0)
        def _():
            prepare(p)

        at = pl.ds(pl.multiple_of(2 * p * half, 2 * half), 2 * half)

        def weights(side):
            scores = scale * lax.dot_general(
                stacked[tile, side * group : (side + 1) * group, :], keys[at, :],
                (((1,), (1,)), ((), ())), preferred_element_type=F32,
            )
            return jnp.exp2(scores).astype(BF16)

        def add(side, parts):
            accum[tile, side * group : (side + 1) * group, :] += jnp.dot(
                parts, vals[side, at, :], preferred_element_type=F32
            )

        parts_a = weights(0)
        parts_b = weights(1)
        add(0, parts_a)
        add(1, parts_b)
        return carry

    lax.fori_loop(0, 4 * tiles, advance, 0)
    for t in range(tiles):
        numerator, sums = collect(accum[t], tq, width)
        num_ref[t * tq : (t + 1) * tq, :] = numerator
        sum_ref[t * tq : (t + 1) * tq, :] = sums
    for n in (5, 14, 15, 16, 17):
        moves[n].wait_recv()
    for copy in exchanges + moves:
        copy.wait_send()
    for copy in [keep] + own_out:
        copy.wait()
    for p in range(4):
        for copy in hand_over(p):
            copy.wait()


def attend_kernel(
    tq, big, small,
    late_hbm, first_keys, first_a, first_b, query_hbm, raw_hbm, num_hbm, sum_hbm, wqkv_hbm,
    wout_hbm, whid_hbm, wback_hbm, note_ref, first_top, gain2_ref, out_ref,
    late, query, raw, num, sums_in, wkv, wout, whid, wback,
    keys, vals_a, vals_b, stacked, accum, top, key_top, sems,
):
    loops, half, width = late_hbm.shape
    slots = query_hbm.shape[0]
    head = width // HEADS
    kt = min(256, half)
    early_rows = loops * half
    scale = math.log2(math.e) / math.sqrt(head)
    me = lax.axis_index("loop")

    pairs = [(wqkv_hbm.at[:, pl.ds(width, 2 * width)], wkv)]
    pairs += [(late_hbm.at[j], late.at[j]) for j in range(loops)]
    pairs += [(query_hbm, query), (raw_hbm, raw), (num_hbm, num), (sum_hbm, sums_in)]
    pairs += [(wout_hbm, wout), (whid_hbm, whid), (wback_hbm, wback)]
    front = pl.ds(0, early_rows)
    pairs += [
        (first_keys, keys.at[front]), (first_a, vals_a.at[front]), (first_b, vals_b.at[front]),
    ]
    loads = [pltpu.make_async_copy(src, dst, sems.at[n]) for n, (src, dst) in enumerate(pairs)]
    for load in loads:
        load.start()
    out_ref[...] = jnp.zeros_like(out_ref)
    key_top[...] = first_top[...]

    def live_rows(j):
        note = note_ref[j].astype(F32)
        high, low = jnp.max(note[:, :128]), jnp.max(note[:, 128:])
        return (high * 128.0 + low).astype(jnp.int32)

    counts = [live_rows(j) for j in range(loops)]
    loads[0].wait()
    base = jnp.int32(early_rows)
    for j in range(loops):
        loads[1 + j].wait()
        count = jnp.maximum(counts[j] - half, 0)

        def tile(t, carry, j=j, base=base, count=count):
            start = pl.multiple_of(t * kt, kt)
            valid = iota((kt, width), 0) + start < count
            k, va, vb, peak = project(late[j, pl.ds(start, kt), :], wkv[...], valid, width)
            at = pl.ds(pl.multiple_of(base + start, 16), kt)
            keys[at, :] = k
            vals_a[at, :] = va
            vals_b[at, :] = vb
            key_top[...] = jnp.maximum(key_top[...], peak)
            return carry

        lax.fori_loop(0, pl.cdiv(count, kt), tile, 0)
        base = base + pl.cdiv(count, 16) * 16

    total_rows = base
    tail = pl.ds(pl.multiple_of(total_rows, 16), small)
    for ref in (keys, vals_a, vals_b):
        ref[tail, :] = jnp.zeros((small, width), BF16)
    highest = jnp.max(key_top[...], axis=0, keepdims=True)
    for load in loads[1 + loops : -3]:
        load.wait()

    mine = live_rows(me)
    to_head = one_hot(iota((width, 128), 0) // head == iota((width, 128), 1))
    flag_lane = one_hot(iota((8, width), 1) == head)
    reach = (jnp.abs(query[...].astype(F32)) * highest).astype(BF16)
    bound = jnp.max(jnp.dot(reach, to_head, preferred_element_type=F32))
    unshifted = bound * (1.02 * scale) < 90.0

    def wait_early(condition):
        @pl.when(condition)
        def _():
            for load in loads[-3:]:
                load.wait()

    wait_early(jnp.logical_not(unshifted))

    def queries(tq, start):
        group = HEADS // 2 * tq
        at_q = pl.ds(start, tq)
        q = query[at_q, :]
        lane_head = iota((tq, width), 1) // head
        for n, h in enumerate(head_order()):
            stacked[n * tq : (n + 1) * tq, :] = jnp.where(lane_head == h, q, jnp.zeros_like(q))
        accum[: 2 * group, :] = jnp.zeros((2 * group, width), F32)
        halves = ((slice(0, group), vals_a), (slice(group, 2 * group), vals_b))
        begun = jnp.logical_and(unshifted, start < half)
        first = jnp.where(begun, early_rows, 0)
        blocks = pl.cdiv(total_rows - first, small)

        def scores(at, rows):
            return scale * lax.dot_general(
                stacked[rows, :], keys[at, :], (((1,), (1,)), ((), ())), preferred_element_type=F32
            )

        def plain(size, offset):
            at = pl.ds(pl.multiple_of(offset, 16), size)
            parts = [jnp.exp2(scores(at, rows)).astype(BF16) for rows, vals in halves]
            for (rows, vals), part in zip(halves, parts):
                accum[rows, :] += jnp.dot(part, vals[at, :], preferred_element_type=F32)

        def shifted(j, carry):
            at = pl.ds(pl.multiple_of(j * small, small), small)
            flags = lax.dot_general(
                flag_lane, vals_a[at, :], (((1,), (1,)), ((), ())), preferred_element_type=F32
            )
            live = flags[0:1, :] > 0.5
            for rows, vals in halves:
                values = jnp.where(live, scores(at, rows), -1e30)
                old = top[rows, :]
                new = jnp.maximum(old, jnp.max(values, axis=1, keepdims=True))
                top[rows, :] = new
                factor = jnp.exp2(old - new)
                weights = jnp.exp2(values - new[:, :1]).astype(BF16)
                accum[rows, :] = accum[rows, :] * factor[:, :1] + jnp.dot(
                    weights, vals[at, :], preferred_element_type=F32
                )
            return carry

        @pl.when(unshifted)
        def _():
            per = big // small
            many = blocks // per

            def step(j, carry):
                plain(big, first + j * big)
                return carry

            lax.fori_loop(0, many, step, 0)
            left = blocks - many * per
            offset = first + many * big
            size = big // 2
            while size >= small:
                units = size // small
                taken = left >= units

                @pl.when(taken)
                def _(size=size, offset=offset):
                    plain(size, offset)

                left = jnp.where(taken, left - units, left)
                offset = jnp.where(taken, offset + size, offset)
                size //= 2

        @pl.when(jnp.logical_not(unshifted))
        def _():
            top[: 2 * group, :] = jnp.full((2 * group, 128), -1e30, F32)
            lax.fori_loop(0, blocks, shifted, 0)

        numerator, sums = collect(accum[: 2 * group, :], tq, width)
        at_p = pl.ds(pl.multiple_of(jnp.where(start < half, start, 0), 16), tq)
        numerator = numerator + jnp.where(begun, num[at_p, :], 0.0)
        sums = sums + jnp.where(begun, sums_in[at_p, :], 0.0)
        even = even_lane((tq, width), head)
        total = jnp.where(
            even, pltpu.roll(sums, width - head, 1), pltpu.roll(sums, head, 1)
        )
        attended = (numerator / total).astype(BF16)
        mixed = raw[at_q, :].astype(F32) + jnp.dot(
            attended, wout[...], preferred_element_type=F32
        )
        normed2 = normalize(mixed, gain2_ref[...]).astype(BF16)
        inner = jnp.dot(normed2, whid[...], preferred_element_type=F32)
        hidden = (0.5 * inner * (1.0 + lax.erf(inner * math.sqrt(0.5)))).astype(BF16)
        result = mixed + jnp.dot(hidden, wback[...], preferred_element_type=F32)
        out_ref[at_q, :] = result.astype(BF16)

    tiles = pl.cdiv(mine, tq)
    begun_tiles = half // tq

    def each_tile(i, carry):
        wait_early(jnp.logical_and(unshifted, i == begun_tiles))
        queries(tq, pl.multiple_of(i * tq, tq))
        return carry

    lax.fori_loop(0, tiles, each_tile, 0)
    wait_early(jnp.logical_and(unshifted, tiles <= begun_tiles))


def give_back_kernel(
    regions, loops, result_ref, rank_ref, place_ref, out_ref, outbox, inbox, send, recv
):
    rows = out_ref.shape[0]
    chunk = CAP * loops
    slots = regions * chunk
    region, loop = lax.axis_index("region"), lax.axis_index("loop")
    barrier = pltpu.get_barrier_semaphore()
    for k in range(1, regions):
        pl.semaphore_signal(
            barrier, inc=1, device_id=(lax.rem(region + k, regions), loop), device_id_type=MESH
        )

    def column(row_ref):
        size = row_ref.shape[1]
        row = jnp.broadcast_to(row_ref[0:1, :].astype(F32), (128, size))
        return row.T[:, 0:1].astype(jnp.int32)

    unpack = one_hot(column(rank_ref) == iota((slots, slots), 1))
    outbox[...] = jnp.dot(unpack, result_ref[...], preferred_element_type=F32).astype(BF16)
    pl.semaphore_wait(barrier, regions - 1)

    def exchange(k):
        peer = lax.rem(region + k, regions)
        return pltpu.make_async_remote_copy(
            src_ref=outbox.at[pl.ds(pl.multiple_of(peer * chunk, chunk), chunk)],
            dst_ref=inbox.at[pl.ds(pl.multiple_of(region * chunk, chunk), chunk)],
            send_sem=send.at[k],
            recv_sem=recv.at[k],
            device_id=(peer, loop),
            device_id_type=MESH,
        )

    exchanges = [exchange(k) for k in range(1, regions)]
    for copy in exchanges:
        copy.start()
    own = pl.ds(pl.multiple_of(region * chunk, chunk), chunk)
    inbox[own, :] = outbox[own, :]
    take = one_hot(column(place_ref) == iota((rows, slots), 1))
    for copy in exchanges:
        copy.wait_recv()
    out_ref[...] = jnp.dot(take, inbox[...], preferred_element_type=F32).astype(BF16)
    for copy in exchanges:
        copy.wait_send()


def local(
    tiles, tokens, dest, norm1_gain, w_qkv, w_out, norm2_gain, w_hidden, w_back
):
    tq, big, small = tiles
    rows, width = tokens.shape
    regions, loops = lax.axis_size("region"), lax.axis_size("loop")
    chunk = CAP * loops
    slots = regions * chunk
    half = slots // 2
    vmem = pl.BlockSpec(memory_space=pltpu.VMEM)
    hbm = pl.BlockSpec(memory_space=pltpu.HBM)
    full = 62 * 1024 * 1024
    params = pltpu.CompilerParams
    shape = jax.ShapeDtypeStruct
    (
        late, first_keys, first_a, first_b, query, raw, notes, num, sums, key_top, place, rank,
    ) = pl.pallas_call(
        functools.partial(route_kernel, regions, loops, tq),
        out_shape=(
            shape((loops, half, width), BF16),
            shape((loops * half, width), BF16),
            shape((loops * half, width), BF16),
            shape((loops * half, width), BF16),
            shape((slots, width), BF16),
            shape((slots, width), BF16),
            shape((loops, EXTRA, width), BF16),
            shape((half, width), F32),
            shape((half, width), F32),
            shape((8, width), F32),
            shape((8, rows), jnp.int32),
            shape((8, slots), jnp.int32),
        ),
        in_specs=[vmem] * 4,
        out_specs=(hbm,) * 6 + (vmem,) * 6,
        scratch_shapes=[
            pltpu.VMEM((slots, width), BF16),
            pltpu.VMEM((slots, width), BF16),
            pltpu.VMEM((slots, width), BF16),
            pltpu.VMEM((slots, width), BF16),
            pltpu.VMEM((loops, half + EXTRA, width), BF16),
            pltpu.VMEM((half, width), BF16),
            pltpu.VMEM((loops * half, width), BF16),
            pltpu.VMEM((2, loops * half, width), BF16),
            pltpu.VMEM((half // tq, HEADS * tq, width), BF16),
            pltpu.VMEM((half // tq, HEADS * tq, width), F32),
            pltpu.SemaphoreType.DMA((regions,)),
            pltpu.SemaphoreType.DMA((regions,)),
            pltpu.SemaphoreType.DMA((18,)),
            pltpu.SemaphoreType.DMA((18,)),
            pltpu.SemaphoreType.DMA((15,)),
        ],
        compiler_params=params(vmem_limit_bytes=full, collective_id=0, has_side_effects=True),
        name="route",
    )(tokens, dest.reshape(1, rows), norm1_gain.reshape(1, width), w_qkv)
    key_rows = loops * slots + small + min(256, half)
    result = pl.pallas_call(
        functools.partial(attend_kernel, *tiles),
        out_shape=shape((slots, width), BF16),
        in_specs=[hbm] * 12 + [vmem] * 3,
        out_specs=vmem,
        scratch_shapes=[
            pltpu.VMEM((loops, half, width), BF16),
            pltpu.VMEM((slots, width), BF16),
            pltpu.VMEM((slots, width), BF16),
            pltpu.VMEM((half, width), F32),
            pltpu.VMEM((half, width), F32),
            pltpu.VMEM((width, 2 * width), BF16),
            pltpu.VMEM(w_out.shape, BF16),
            pltpu.VMEM(w_hidden.shape, BF16),
            pltpu.VMEM(w_back.shape, BF16),
            pltpu.VMEM((key_rows, width), BF16),
            pltpu.VMEM((key_rows, width), BF16),
            pltpu.VMEM((key_rows, width), BF16),
            pltpu.VMEM((HEADS * tq, width), BF16),
            pltpu.VMEM((HEADS * tq, width), F32),
            pltpu.VMEM((HEADS * tq, 128), F32),
            pltpu.VMEM((8, width), F32),
            pltpu.SemaphoreType.DMA((loops + 11,)),
        ],
        compiler_params=params(vmem_limit_bytes=full),
        name="attend",
    )(
        late, first_keys, first_a, first_b, query, raw, num, sums, w_qkv, w_out, w_hidden,
        w_back, notes, key_top, norm2_gain.reshape(1, width),
    )
    return pl.pallas_call(
        functools.partial(give_back_kernel, regions, loops),
        out_shape=jax.ShapeDtypeStruct((rows, width), BF16),
        in_specs=[vmem] * 3,
        out_specs=vmem,
        scratch_shapes=[
            pltpu.VMEM((slots, width), BF16),
            pltpu.VMEM((slots, width), BF16),
            pltpu.SemaphoreType.DMA((regions,)),
            pltpu.SemaphoreType.DMA((regions,)),
        ],
        compiler_params=params(vmem_limit_bytes=32 * 1024 * 1024, collective_id=1, has_side_effects=True),
        name="give_back",
    )(result, rank, place)


def build(mesh, tiles):
    spread = P(("region", "loop"), None)
    return jax.shard_map(
        functools.partial(local, tiles),
        mesh=mesh,
        in_specs=(spread, spread) + (P(),) * 6,
        out_specs=spread,
        check_vma=False,
    )


def solution(mesh):
    return build(mesh, (256, 2048, 256))
```
